128 devices in a mesh: phase: 2 (over core), blk: 64 (over x, y, z).
Axes of the slice: x: 4, y: 4, z: 4, core: 2. Of those that a mesh axis runs over, the one named last changes fastest.
Arguments:
- normals: bfloat16 [128, 65536], P(None, 'blk'), may hold values from -6 to 6
- section_tile_list: bfloat16 [2, 1280, 512, 512], P('phase', 'blk'), may hold values from -0.078125 to 0.078125
- tile_output_block: int32 [2, 1280], P('phase'), may hold values from 0 to 127, as said below
- tile_col: int32 [2, 1280], P('phase', 'blk'), may hold values from 0 to 1
- notional: float32 [65536], P('blk'), may hold values from 1 to 8
- strike: float32 [65536], P('blk'), may hold values from -4 to 4
Outputs:
- tile_sens: bfloat16 [2, 1280, 512, 512], P('phase', 'blk')
- input_adjoint: bfloat16 [2, 128, 65536], P('phase', None, 'blk')
The draws below stay inside these ranges and needn't reach their ends.
Inputs may be any that keep to these rules, and one draw needn't show every extreme that they name: Within one section, the 20 tiles of one index i of blk (tiles i * 20 to i * 20 + 19) have output blocks on distinct indices of blk, index = tile_output_block // 2.
All inputs are finite; a program needn't handle non-finite values.
Results may differ from the reference program's by a relative error of at most 0.008.
Values may be sent and summed in bfloat16 or wider, within the bound.
No kernel may reach another device: no remote copies, remote signals or barrier semaphores. Data moves between devices by JAX's collectives and lax.ppermute only.
A program may use at most 256 MiB of HBM per device.

```python
import math
import jax
import jax.numpy as jnp
from jax import lax

F = 65536
BS = 512
SCEN = 128
NB = 128
FB_DEV = 2
SLOTS = 20
N_BLK = 64


def draw_tile_output_block(key, part):
    first_key = jax.random.fold_in(key, 11)
    second_key = jax.random.fold_in(key, 12)
    third_key = jax.random.fold_in(key, 13)
    hotness = jax.random.randint(first_key, (2, 1, N_BLK), 0, 4)
    noise_part = jax.random.randint(second_key, (2, N_BLK, N_BLK), 0, 2 * N_BLK)
    owner_ids = jnp.arange(N_BLK, dtype=jnp.int32)[None, None, :]
    scores = (noise_part + hotness * N_BLK) * N_BLK + owner_ids
    _, owners = lax.top_k(scores, SLOTS)
    inner_block = jax.random.randint(third_key, (2, N_BLK, SLOTS), 0, FB_DEV)
    rows_drawn = owners.astype(jnp.int32) * FB_DEV + inner_block
    return rows_drawn.reshape(2, N_BLK * SLOTS).astype(jnp.int32)


def plant(result, own_key, smallest, top_value):
    place = [jax.random.randint(jax.random.fold_in(own_key, axis), (), 0, length) for axis, length in enumerate(result.shape)]
    main_axis = result.shape.index(max(result.shape))
    beside = place[:main_axis] + [(place[main_axis] + 1) % result.shape[main_axis]] + place[main_axis + 1:]
    return result.at[tuple(place)].set(smallest).at[tuple(beside)].set(top_value)


def block_levels(key, extent, pieces, least, top_value):
    factor_of = 1.0
    for position, parts in pieces:
        draws = jax.random.uniform(jax.random.fold_in(jax.random.fold_in(key, 6), position), (parts,), jnp.float32, least / len(pieces), top_value / len(pieces))
        factor_of = factor_of * jnp.repeat(jnp.exp(draws), extent[position] // parts).reshape((-1,) + (1,) * (len(extent) - 1 - position))
    return factor_of


def centred(stream_key, extent, deviation, limit, shards=(), kind=jnp.bfloat16):
    values = deviation * jax.random.normal(stream_key, extent, jnp.float32)
    if shards:
        values = values * block_levels(stream_key, extent, shards, -0.22, 0.18)
    return jnp.clip(values, -limit, limit).astype(kind)


def setup_inputs(seed: int = 0) -> dict:
    key_of = jax.random.split(jax.random.key(seed), 7)
    return {
        "normals": centred(key_of[0], (SCEN, F), 1.0, 6.0, ((1, 64),)),
        "section_tile_list": centred(key_of[1], (2, N_BLK * SLOTS, BS, BS), (BS * max(1, N_BLK * SLOTS // NB)) ** -0.5, 0.078125, ((0, 2), (1, 64))),
        "tile_output_block": draw_tile_output_block(jax.random.fold_in(key_of[6], 71), 0),
        "tile_col": plant(jax.random.randint(key_of[3], (2, N_BLK * SLOTS), 0, FB_DEV), jax.random.fold_in(key_of[3], 1), 0, FB_DEV - 1).astype(jnp.int32),
        "notional": jnp.clip(jnp.exp(math.log(8.0) - 2.0794415 * jax.random.uniform(key_of[4], (F,), jnp.float32) ** block_levels(key_of[4], (F,), ((0, 64),), -0.2, 0.2)), 1.0, 8.0),
        "strike": centred(key_of[5], (F,), 1.0, 4.0, ((0, 64),), jnp.float32),
    }


def section_forward_pass(inputs, tiles, rows, cols):
    blocks = inputs.reshape(SCEN, NB, BS)
    tile_items = (tiles.reshape(N_BLK, SLOTS, BS, BS), rows.reshape(N_BLK, SLOTS), cols.reshape(N_BLK, SLOTS))

    def accumulate(total, tile_entry):
        tile_g, row_g, col_g = tile_entry
        picked = jnp.take(blocks, col_g, axis=1).astype(jnp.float32)
        products = jnp.einsum('stk,tkn->tsn', picked, tile_g.astype(jnp.float32)).astype(jnp.bfloat16)
        products = lax.optimization_barrier(products).astype(jnp.float32)
        return (total + jax.ops.segment_sum(products, row_g, NB), None)
    total, _ = lax.scan(accumulate, jnp.zeros((NB, SCEN, BS), jnp.float32), tile_items)
    return jnp.transpose(total, (1, 0, 2)).reshape(SCEN, F)

def section_backward(inputs, tiles, rows, cols, grads):
    in_blocks = inputs.reshape(SCEN, NB, BS)
    grad_blocks = grads.reshape(SCEN, NB, BS)
    tile_items = (tiles.reshape(N_BLK, SLOTS, BS, BS), rows.reshape(N_BLK, SLOTS), cols.reshape(N_BLK, SLOTS))

    def accumulate(total, tile_entry):
        tile_g, row_g, col_g = tile_entry
        picked_in = jnp.take(in_blocks, col_g, axis=1).astype(jnp.float32)
        picked_grad = jnp.take(grad_blocks, row_g, axis=1).astype(jnp.float32)
        sensitivity = jnp.einsum('stk,stn->tkn', picked_in, picked_grad)
        in_grads = jnp.einsum('stn,tkn->tsk', picked_grad, tile_g.astype(jnp.float32))
        return (total + jax.ops.segment_sum(in_grads, col_g, NB), sensitivity)
    total, sensitivity = lax.scan(accumulate, jnp.zeros((NB, SCEN, BS), jnp.float32), tile_items)
    in_grads = jnp.transpose(total, (1, 0, 2)).reshape(SCEN, F)
    return (sensitivity.reshape(N_BLK * SLOTS, BS, BS), in_grads)

def reference(normals, section_tile_list, tile_output_block, tile_col, notional, strike):
    holder_base = jnp.arange(N_BLK * SLOTS, dtype=jnp.int32) // SLOTS * FB_DEV
    global_column_ids = (holder_base[None, :] + tile_col).astype(jnp.int32)
    market_shock_draws = section_forward_pass(normals, section_tile_list[0], tile_output_block[0], global_column_ids[0]).astype(jnp.bfloat16)
    valued_paths = section_forward_pass(market_shock_draws, section_tile_list[1], tile_output_block[1], global_column_ids[1])
    scenario_path_weight = 1.0 / math.sqrt(SCEN)
    valuation_gradient = (notional[None, :] * jax.nn.sigmoid(valued_paths - strike[None, :]) * scenario_path_weight).astype(jnp.bfloat16)
    sens_one, shock_grads = section_backward(market_shock_draws, section_tile_list[1], tile_output_block[1], global_column_ids[1], valuation_gradient)
    shock_grads = shock_grads.astype(jnp.bfloat16)
    sens_zero, normal_grads = section_backward(normals, section_tile_list[0], tile_output_block[0], global_column_ids[0], shock_grads)
    tile_sens = jnp.stack([sens_zero, sens_one]).astype(jnp.bfloat16)
    input_adjoint = jnp.stack([normal_grads.astype(jnp.bfloat16), shock_grads])
    return (tile_sens, input_adjoint)
```

```python
import functools
import math

import jax
import jax.numpy as jnp
from jax import lax
from jax.experimental import pallas as pl
from jax.experimental.pallas import tpu as pltpu
from jax.sharding import PartitionSpec as P

SLICE = 8
VMEM_LIMIT = 48 * 1024 * 1024


def params(**kw):
    return pltpu.CompilerParams(vmem_limit_bytes=VMEM_LIMIT, **kw)


def products_body(cols, x, tiles, out, *, first, width):
    step = pl.program_id(0)
    parts = []
    for u in range(2):
        col = cols[first + 2 * step + u]
        picked = x[:, pl.ds(pl.multiple_of(col * width, width), width)]
        product = jnp.dot(picked, tiles[u], preferred_element_type=jnp.float32)
        parts.append(product.T.reshape(width // SLICE, SLICE, x.shape[0]))
    both = jnp.concatenate(parts, axis=1).astype(jnp.bfloat16)
    out[:, pl.ds(pl.multiple_of(2 * SLICE * step, 2 * SLICE), 2 * SLICE), :] = both


def products(cols, x, tiles, first, count):
    width = tiles.shape[1]
    scen = x.shape[0]
    return pl.pallas_call(
        functools.partial(products_body, first=first, width=width),
        grid=(count // 2,),
        in_specs=[
            pl.BlockSpec(memory_space=pltpu.SMEM),
            pl.BlockSpec(x.shape, lambda g: (0, 0)),
            pl.BlockSpec((2, width, width), lambda g: (g + first // 2, 0, 0)),
        ],
        out_specs=pl.BlockSpec((width // SLICE, count * SLICE, scen), lambda g: (0, 0, 0)),
        out_shape=jax.ShapeDtypeStruct((width // SLICE, count * SLICE, scen), jnp.bfloat16),
        compiler_params=params(),
        name="products",
    )(cols, x, tiles)


def add_up_body(idx, data, out, *, count):
    out[...] = jnp.zeros_like(out)

    @pl.loop(0, data.shape[0])
    def _(i):
        values = data[i].astype(jnp.float32)
        places = [idx[i * count + t] for t in range(count)]
        sums = [
            out[places[t]] + values[t * SLICE : (t + 1) * SLICE] for t in range(count)
        ]
        for t in range(count):
            out[places[t]] = sums[t]


def add_up(idx, data, blocks):
    count = data.shape[1] // SLICE
    return pl.pallas_call(
        functools.partial(add_up_body, count=count),
        in_specs=[pl.BlockSpec(memory_space=pltpu.SMEM), pl.BlockSpec(memory_space=pltpu.VMEM)],
        out_specs=pl.BlockSpec(memory_space=pltpu.VMEM),
        out_shape=jax.ShapeDtypeStruct((blocks, SLICE, data.shape[2]), jnp.float32),
        compiler_params=params(),
        name="add_up",
    )(idx, data)


def hand_out(idx, held, out, count):
    @pl.loop(0, out.shape[0])
    def _(i):
        for t in range(0, count, 2):
            pair = [held[idx[i * count + t]], held[idx[i * count + t + 1]]]
            rows = jnp.concatenate(pair, axis=0).astype(jnp.bfloat16)
            out[i, t * SLICE : (t + 2) * SLICE, :] = rows


def value_and_hand_out_body(idx, mine, other, notional, strike, out, held, *, count, weight):
    @pl.loop(0, held.shape[0], step=8)
    def _(b):
        for k in range(8):
            moneyness = mine[b + k] + other[b + k]
            held[b + k] = notional[b + k] * jax.nn.sigmoid(moneyness - strike[b + k]) * weight

    hand_out(idx, held, out, count)


def value_and_hand_out(idx, mine, other, notional, strike, shards, count, weight):
    scen = mine.shape[2]
    vmem = pl.BlockSpec(memory_space=pltpu.VMEM)
    return pl.pallas_call(
        functools.partial(value_and_hand_out_body, count=count, weight=weight),
        in_specs=[pl.BlockSpec(memory_space=pltpu.SMEM), vmem, vmem, vmem, vmem],
        out_specs=vmem,
        out_shape=jax.ShapeDtypeStruct((shards, count * SLICE, scen), jnp.bfloat16),
        scratch_shapes=[pltpu.VMEM(mine.shape, jnp.float32)],
        compiler_params=params(),
        name="value_and_hand_out",
    )(idx, mine, other, notional, strike)


def only_hand_out_body(idx, blocks, out, held, *, count):
    held[...] = blocks[...].astype(jnp.float32).reshape(held.shape)
    hand_out(idx, held, out, count)


def only_hand_out(idx, blocks, shards, count):
    scen = blocks.shape[2]
    vmem = pl.BlockSpec(memory_space=pltpu.VMEM)
    held = blocks.shape[0] * blocks.shape[1] // SLICE
    return pl.pallas_call(
        functools.partial(only_hand_out_body, count=count),
        in_specs=[pl.BlockSpec(memory_space=pltpu.SMEM), vmem],
        out_specs=vmem,
        out_shape=jax.ShapeDtypeStruct((shards, count * SLICE, scen), jnp.bfloat16),
        scratch_shapes=[pltpu.VMEM((held, SLICE, scen), jnp.float32)],
        compiler_params=params(),
        name="hand_out",
    )(idx, blocks)


def tile_grad_pair(grads, pair):
    rows = grads[:, pl.ds(pl.multiple_of(pair * 2 * SLICE, 2 * SLICE), 2 * SLICE), :]
    rows = rows.astype(jnp.float32)
    width = rows.shape[0] * SLICE
    return [
        rows[:, u * SLICE : (u + 1) * SLICE, :].reshape(width, -1).astype(jnp.bfloat16)
        for u in range(2)
    ]


def first_backward_body(cols, low, high, tiles, out, total, *, half):
    step = pl.program_id(0)

    @pl.when(step == 0)
    def _():
        total[...] = jnp.zeros_like(total)

    def go(grads, pair):
        for u, grad in enumerate(tile_grad_pair(grads, pair)):
            total[cols[2 * step + u]] += jnp.dot(tiles[u], grad, preferred_element_type=jnp.float32)

    @pl.when(step < half // 2)
    def _():
        go(low, step)

    @pl.when(step >= half // 2)
    def _():
        go(high, step - half // 2)

    @pl.when(step == pl.num_programs(0) - 1)
    def _():
        out[...] = total[...].astype(jnp.bfloat16)


def first_backward(cols, low, high, tiles, blocks_dev):
    slots, width, _ = tiles.shape
    scen = low.shape[2]
    whole = pl.BlockSpec(low.shape, lambda g: (0, 0, 0))
    return pl.pallas_call(
        functools.partial(first_backward_body, half=slots // 2),
        grid=(slots // 2,),
        in_specs=[
            pl.BlockSpec(memory_space=pltpu.SMEM),
            whole,
            whole,
            pl.BlockSpec((2, width, width), lambda g: (g, 0, 0)),
        ],
        out_specs=pl.BlockSpec((blocks_dev, width, scen), lambda g: (0, 0, 0)),
        out_shape=jax.ShapeDtypeStruct((blocks_dev, width, scen), jnp.bfloat16),
        scratch_shapes=[pltpu.VMEM((blocks_dev, width, scen), jnp.float32)],
        compiler_params=params(),
        name="first_backward",
    )(cols, low, high, tiles)


def last_backward_body(
    meta, low0, high0, low1, high1, inputs, tiles, sens, adjoint, total, *, half
):
    step = pl.program_id(0)
    section = meta[2 * half]

    @pl.when(step == 0)
    def _():
        total[...] = jnp.zeros_like(total)

    def go(grads, pair):
        for u, grad in enumerate(tile_grad_pair(grads, pair)):
            col = meta[2 * step + u]
            total[col] += jnp.dot(tiles[u], grad, preferred_element_type=jnp.float32)
            sens[u] = lax.dot_general(
                inputs[col], grad, (((1,), (1,)), ((), ())), preferred_element_type=jnp.float32
            ).astype(jnp.bfloat16)

    for wanted, low, high in ((0, low0, high0), (1, low1, high1)):

        @pl.when((section == wanted) & (step < half // 2))
        def _(low=low):
            go(low, step)

        @pl.when((section == wanted) & (step >= half // 2))
        def _(high=high):
            go(high, step - half // 2)

    @pl.when(step == pl.num_programs(0) - 1)
    def _():
        width = total.shape[1]
        for c in range(total.shape[0]):
            adjoint[:, c * width : (c + 1) * width] = total[c].T.astype(jnp.bfloat16)


def last_backward(meta, low0, high0, low1, high1, inputs, tiles):
    slots, width, _ = tiles.shape
    scen = low0.shape[2]
    blocks_dev = inputs.shape[0]
    whole = pl.BlockSpec(low0.shape, lambda g: (0, 0, 0), pipeline_mode=pl.Buffered(1))
    pair = pl.BlockSpec((2, width, width), lambda g: (g, 0, 0))
    return pl.pallas_call(
        functools.partial(last_backward_body, half=slots // 2),
        grid=(slots // 2,),
        in_specs=[
            pl.BlockSpec(memory_space=pltpu.SMEM),
            whole,
            whole,
            whole,
            whole,
            pl.BlockSpec(inputs.shape, lambda g: (0, 0, 0)),
            pair,
        ],
        out_specs=[pair, pl.BlockSpec((scen, blocks_dev * width), lambda g: (0, 0))],
        out_shape=[
            jax.ShapeDtypeStruct(tiles.shape, jnp.bfloat16),
            jax.ShapeDtypeStruct((scen, blocks_dev * width), jnp.bfloat16),
        ],
        scratch_shapes=[pltpu.VMEM((blocks_dev, width, scen), jnp.float32)],
        compiler_params=params(),
        name="last_backward",
    )(meta, low0, high0, low1, high1, inputs, tiles)


def three_terms(values):
    terms = []
    for _ in range(3):
        term = lax.reduce_precision(values, 8, 7)
        terms.append(term)
        values = values - term
    return jnp.stack(terms)


def exchange(block):
    return lax.all_to_all(block, "blk", split_axis=0, concat_axis=0, tiled=True)


def on_device(normals, section_tile_list, tile_output_block, tile_col, notional, strike):
    shards = lax.axis_size("blk")
    core = lax.axis_index("phase")
    tiles = section_tile_list[0]
    slots, width, _ = tiles.shape
    half = slots // 2
    scen, local_width = normals.shape
    blocks_dev = local_width // width
    blocks = shards * blocks_dev
    cols = tile_col[0]
    weight = 1.0 / math.sqrt(scen)

    def of_core(zero, one):
        return jnp.where(core == 0, zero, one)

    def send(block, source):
        return lax.ppermute(block, "phase", [(source, 1 - source)])

    def swap(block):
        return lax.ppermute(block, "phase", [(0, 1), (1, 0)])

    my_rows = tile_output_block[0]
    other_rows = swap(my_rows)
    split_rows = [
        of_core(r.reshape(shards, slots)[:, :half], r.reshape(shards, slots)[:, half:]).reshape(-1)
        for r in (of_core(my_rows, other_rows), of_core(other_rows, my_rows))
    ]

    sent = send(products(cols, normals, tiles, half, half), 0)
    kept = products(cols, normals, tiles, 0, half)
    arrived = exchange(of_core(kept, sent))
    part = add_up(split_rows[0], arrived, blocks)
    shock_slices = (part + swap(part)).astype(jnp.bfloat16)

    scales = jnp.stack([three_terms(notional), three_terms(strike)])
    scales = scales.reshape(6, blocks_dev, shards, SLICE).transpose(2, 0, 1, 3)
    scales = scales.reshape(shards, 1, 6 * blocks_dev * SLICE).astype(jnp.bfloat16)
    scales = jnp.pad(scales, ((0, 0), (0, SLICE - 1), (0, scen - scales.shape[2])))
    shock_rows = shock_slices.reshape(shards, blocks_dev * SLICE, scen)
    arrived = exchange(jnp.concatenate([shock_rows, scales], axis=1))
    shocks = arrived[:, : blocks_dev * SLICE].reshape(shards, blocks_dev, SLICE, scen)
    shocks = shocks.transpose(1, 0, 2, 3).reshape(blocks_dev, width, scen)
    shocks_natural = shocks.transpose(2, 0, 1).reshape(scen, local_width)
    scales = arrived[:, blocks_dev * SLICE, : 6 * blocks_dev * SLICE].astype(jnp.float32)
    scales = scales.reshape(shards, 2, 3, blocks_dev, SLICE)
    scales = (scales[:, :, 0] + scales[:, :, 1]) + scales[:, :, 2]
    scales = scales.transpose(1, 0, 2, 3).reshape(2, blocks, SLICE, 1)

    sent = send(products(cols, shocks_natural, tiles, 0, half), 1)
    kept = products(cols, shocks_natural, tiles, half, half)
    arrived = exchange(of_core(sent, kept))
    part = add_up(split_rows[1], arrived, blocks)
    outgoing = value_and_hand_out(
        split_rows[1], part, swap(part), scales[0], scales[1], shards, half, weight
    )

    high1 = exchange(outgoing)
    low1 = send(high1, 0)
    shock_grad = first_backward(cols, low1, high1, tiles, blocks_dev)

    shock_grad = of_core(send(shock_grad, 1), shock_grad)
    shock_grad = shock_grad.reshape(blocks_dev, shards, SLICE, scen).transpose(1, 0, 2, 3)
    arrived = exchange(shock_grad.reshape(shards, blocks_dev * SLICE, scen))
    low0 = exchange(only_hand_out(split_rows[0], arrived, shards, half))
    high0 = send(low0, 1)

    normals_held = normals.reshape(scen, blocks_dev, width).transpose(1, 2, 0)
    meta = jnp.concatenate([cols, core[None].astype(jnp.int32)])
    sens, adjoint = last_backward(
        meta, low0, high0, low1, high1, of_core(normals_held, shocks), tiles
    )
    return sens[None], adjoint[None]


def solution(mesh):
    return jax.shard_map(
        on_device,
        mesh=mesh,
        in_specs=(
            P(None, "blk"),
            P("phase", "blk", None, None),
            P("phase", None),
            P("phase", "blk"),
            P("blk"),
            P("blk"),
        ),
        out_specs=(P("phase", "blk", None, None), P("phase", None, "blk")),
        check_vma=False,
    )
```

```python
import functools
import math

import jax
import jax.numpy as jnp
from jax import lax
from jax.experimental import pallas as pl
from jax.experimental.pallas import tpu as pltpu
from jax.sharding import PartitionSpec as P

SLICE = 8
VMEM_LIMIT = 16 * 1024 * 1024
STREAM_LIMIT = 48 * 1024 * 1024


def params(limit=VMEM_LIMIT):
    return pltpu.CompilerParams(vmem_limit_bytes=limit)


def tile_copies(source, first, held, sems):
    def copy(k):
        return pltpu.make_async_copy(
            source.at[pl.ds(first + 2 * k, 2)], held.at[pl.ds(2 * k, 2)], sems.at[k]
        )

    return copy


def tile_scratch(count, width):
    return [pltpu.VMEM((count, width, width), jnp.bfloat16), pltpu.SemaphoreType.DMA((count // 2,))]


def product_pair(cols, at, x, tiles, out, pair):
    width = tiles.shape[1]
    parts = []
    for u in range(2):
        col = cols[at + 2 * pair + u]
        picked = x[:, pl.ds(pl.multiple_of(col * width, width), width)]
        product = jnp.dot(picked, tiles[2 * pair + u], preferred_element_type=jnp.float32)
        parts.append(product.T.reshape(width // SLICE, SLICE, x.shape[0]))
    both = jnp.concatenate(parts, axis=1).astype(jnp.bfloat16)
    out[:, pl.ds(pl.multiple_of(2 * SLICE * pair, 2 * SLICE), 2 * SLICE), :] = both


def first_products_body(cols, x, tiles, out, held, sems, *, first):
    pairs = held.shape[0] // 2
    copy = tile_copies(tiles, first, held, sems)
    for k in range(pairs):
        copy(k).start()

    @pl.loop(0, pairs)
    def _(k):
        copy(k).wait()
        product_pair(cols, first, x, held, out, k)


def first_products(cols, x, tiles, first, count):
    width = tiles.shape[1]
    scen = x.shape[0]
    vmem = pl.BlockSpec(memory_space=pltpu.VMEM)
    return pl.pallas_call(
        functools.partial(first_products_body, first=first),
        in_specs=[
            pl.BlockSpec(memory_space=pltpu.SMEM),
            vmem,
            pl.BlockSpec(memory_space=pl.ANY),
        ],
        out_specs=vmem,
        out_shape=jax.ShapeDtypeStruct((width // SLICE, count * SLICE, scen), jnp.bfloat16),
        scratch_shapes=tile_scratch(count, width),
        compiler_params=params(STREAM_LIMIT),
        name="first_products",
    )(cols, x, tiles)


def start_split_tiles(core, received, tiles, held, sems):
    count = held.shape[0]

    @pl.when(core == 0)
    def _():
        for k in range(count // 2):
            tile_copies(received, 0, held, sems)(k).start()

    @pl.when(core == 1)
    def _():
        for k in range(count // 2):
            tile_copies(tiles, count, held, sems)(k).start()

    return tile_copies(received, 0, held, sems)


def split_products_body(meta, x, received, tiles, out, held, sems):
    copy = start_split_tiles(meta[0], received, tiles, held, sems)

    @pl.loop(0, held.shape[0] // 2)
    def _(k):
        copy(k).wait()
        product_pair(meta, 1, x, held, out, k)


def split_products(meta, x, received, tiles):
    count, width = received.shape[0] // 2, received.shape[1]
    scen = x.shape[0]
    vmem = pl.BlockSpec(memory_space=pltpu.VMEM)
    hbm = pl.BlockSpec(memory_space=pl.ANY)
    return pl.pallas_call(
        split_products_body,
        in_specs=[pl.BlockSpec(memory_space=pltpu.SMEM), vmem, hbm, hbm],
        out_specs=vmem,
        out_shape=jax.ShapeDtypeStruct((width // SLICE, count * SLICE, scen), jnp.bfloat16),
        scratch_shapes=tile_scratch(count, width),
        compiler_params=params(STREAM_LIMIT),
        name="split_products",
    )(meta, x, received, tiles)


def add_up_body(idx, data, out, *, count):
    out[...] = jnp.zeros_like(out)

    @pl.loop(0, data.shape[0])
    def _(i):
        values = data[i].astype(jnp.float32)
        places = [idx[i * count + t] for t in range(count)]
        sums = [
            out[places[t]] + values[t * SLICE : (t + 1) * SLICE] for t in range(count)
        ]
        for t in range(count):
            out[places[t]] = sums[t]


def add_up(idx, data, blocks):
    count = data.shape[1] // SLICE
    return pl.pallas_call(
        functools.partial(add_up_body, count=count),
        in_specs=[pl.BlockSpec(memory_space=pltpu.SMEM), pl.BlockSpec(memory_space=pltpu.VMEM)],
        out_specs=pl.BlockSpec(memory_space=pltpu.VMEM),
        out_shape=jax.ShapeDtypeStruct((blocks, SLICE, data.shape[2]), jnp.float32),
        compiler_params=params(),
        name="add_up",
    )(idx, data)


def hand_out(idx, held, out, count):
    @pl.loop(0, out.shape[0])
    def _(i):
        for t in range(0, count, 2):
            pair = [held[idx[i * count + t]], held[idx[i * count + t + 1]]]
            rows = jnp.concatenate(pair, axis=0).astype(jnp.bfloat16)
            out[i, t * SLICE : (t + 2) * SLICE, :] = rows


def value_and_hand_out_body(idx, mine, other, notional, strike, out, held, *, count, weight):
    @pl.loop(0, held.shape[0], step=8)
    def _(b):
        for k in range(8):
            moneyness = mine[b + k] + other[b + k]
            held[b + k] = notional[b + k] * jax.nn.sigmoid(moneyness - strike[b + k]) * weight

    hand_out(idx, held, out, count)


def value_and_hand_out(idx, mine, other, notional, strike, shards, count, weight):
    scen = mine.shape[2]
    vmem = pl.BlockSpec(memory_space=pltpu.VMEM)
    return pl.pallas_call(
        functools.partial(value_and_hand_out_body, count=count, weight=weight),
        in_specs=[pl.BlockSpec(memory_space=pltpu.SMEM), vmem, vmem, vmem, vmem],
        out_specs=vmem,
        out_shape=jax.ShapeDtypeStruct((shards, count * SLICE, scen), jnp.bfloat16),
        scratch_shapes=[pltpu.VMEM(mine.shape, jnp.float32)],
        compiler_params=params(),
        name="value_and_hand_out",
    )(idx, mine, other, notional, strike)


def only_hand_out_body(idx, blocks, out, held, *, count):
    held[...] = blocks[...].astype(jnp.float32).reshape(held.shape)
    hand_out(idx, held, out, count)


def only_hand_out(idx, blocks, shards, count):
    scen = blocks.shape[2]
    vmem = pl.BlockSpec(memory_space=pltpu.VMEM)
    held = blocks.shape[0] * blocks.shape[1] // SLICE
    return pl.pallas_call(
        functools.partial(only_hand_out_body, count=count),
        in_specs=[pl.BlockSpec(memory_space=pltpu.SMEM), vmem],
        out_specs=vmem,
        out_shape=jax.ShapeDtypeStruct((shards, count * SLICE, scen), jnp.bfloat16),
        scratch_shapes=[pltpu.VMEM((held, SLICE, scen), jnp.float32)],
        compiler_params=params(),
        name="hand_out",
    )(idx, blocks)


def tile_grad_pair(grads, pair):
    rows = grads[:, pl.ds(pl.multiple_of(pair * 2 * SLICE, 2 * SLICE), 2 * SLICE), :]
    rows = rows.astype(jnp.float32)
    width = rows.shape[0] * SLICE
    return [
        rows[:, u * SLICE : (u + 1) * SLICE, :].reshape(width, -1).astype(jnp.bfloat16)
        for u in range(2)
    ]


def split_backward_body(meta, grads, received, tiles, total, held, sems):
    copy = start_split_tiles(meta[0], received, tiles, held, sems)
    total[...] = jnp.zeros_like(total)

    @pl.loop(0, held.shape[0] // 2)
    def _(k):
        copy(k).wait()
        for u, grad in enumerate(tile_grad_pair(grads, k)):
            product = jnp.dot(held[2 * k + u], grad, preferred_element_type=jnp.float32)
            total[meta[1 + 2 * k + u]] += product


def split_backward(meta, grads, received, tiles, blocks_dev):
    count, width = received.shape[0] // 2, received.shape[1]
    vmem = pl.BlockSpec(memory_space=pltpu.VMEM)
    hbm = pl.BlockSpec(memory_space=pl.ANY)
    return pl.pallas_call(
        split_backward_body,
        in_specs=[pl.BlockSpec(memory_space=pltpu.SMEM), vmem, hbm, hbm],
        out_specs=vmem,
        out_shape=jax.ShapeDtypeStruct((blocks_dev, width, grads.shape[2]), jnp.float32),
        scratch_shapes=tile_scratch(count, width),
        compiler_params=params(STREAM_LIMIT),
        name="split_backward",
    )(meta, grads, received, tiles)


def last_backward_body(meta, grads0, grads1, inputs, tiles, *rest, first):
    earlier = rest[:2] if first else ()
    sens, result, grads, total, stage, out_sems, held, sems = rest[len(earlier) :]
    pairs = held.shape[0] // 2
    take = tile_copies(tiles, first, held, sems)
    for k in range(pairs):
        take(k).start()

    @pl.when(meta[0] == 0)
    def _():
        grads[...] = grads0[...]

    @pl.when(meta[0] == 1)
    def _():
        grads[...] = grads1[...]

    total[...] = earlier[0][...] if earlier else jnp.zeros_like(total)

    def put(k):
        slot = lax.rem(k, 2)
        return pltpu.make_async_copy(
            stage.at[slot], sens.at[pl.ds(first + 2 * k, 2)], out_sems.at[slot]
        )

    @pl.loop(0, pairs)
    def _(k):
        @pl.when(k >= 2)
        def _():
            put(k - 2).wait()

        take(k).wait()
        slot = lax.rem(k, 2)
        for u, grad in enumerate(tile_grad_pair(grads, k)):
            col = meta[1 + first + 2 * k + u]
            total[col] += jnp.dot(held[2 * k + u], grad, preferred_element_type=jnp.float32)
            stage[slot, u] = lax.dot_general(
                inputs[col], grad, (((1,), (1,)), ((), ())), preferred_element_type=jnp.float32
            ).astype(jnp.bfloat16)
        put(k).start()

    if earlier:
        width = total.shape[1]
        for c in range(total.shape[0]):
            result[:, c * width : (c + 1) * width] = total[c].T.astype(jnp.bfloat16)
    else:
        result[...] = total[...]
    for k in range(max(pairs - 2, 0), pairs):
        put(k).wait()


def last_backward(meta, grads0, grads1, inputs, tiles, first, count, earlier=()):
    slots, width, _ = tiles.shape
    blocks_dev, _, scen = inputs.shape
    vmem = pl.BlockSpec(memory_space=pltpu.VMEM)
    hbm = pl.BlockSpec(memory_space=pl.ANY)
    result = (
        jax.ShapeDtypeStruct((scen, blocks_dev * width), jnp.bfloat16)
        if earlier
        else jax.ShapeDtypeStruct(inputs.shape, jnp.float32)
    )
    return pl.pallas_call(
        functools.partial(last_backward_body, first=first),
        in_specs=[pl.BlockSpec(memory_space=pltpu.SMEM), vmem, vmem, vmem, hbm]
        + [vmem, hbm][: len(earlier)],
        out_specs=[hbm, vmem],
        out_shape=[jax.ShapeDtypeStruct((slots, width, width), jnp.bfloat16), result],
        scratch_shapes=[
            pltpu.VMEM(grads0.shape, jnp.bfloat16),
            pltpu.VMEM(inputs.shape, jnp.float32),
            pltpu.VMEM((2, 2, width, width), jnp.bfloat16),
            pltpu.SemaphoreType.DMA((2,)),
        ]
        + tile_scratch(count, width),
        input_output_aliases={6: 0} if earlier else {},
        compiler_params=params(STREAM_LIMIT),
        name="last_backward",
    )(meta, grads0, grads1, inputs, tiles, *earlier)


def three_terms(values):
    terms = []
    for _ in range(3):
        term = lax.reduce_precision(values, 8, 7)
        terms.append(term)
        values = values - term
    return jnp.stack(terms)


def exchange(block):
    return lax.all_to_all(block, "blk", split_axis=0, concat_axis=0, tiled=True)


def on_device(normals, section_tile_list, tile_output_block, tile_col, notional, strike):
    shards = lax.axis_size("blk")
    core = lax.axis_index("phase")
    tiles = section_tile_list[0]
    slots, width, _ = tiles.shape
    half = slots // 2
    scen, local_width = normals.shape
    blocks_dev = local_width // width
    blocks = shards * blocks_dev
    cols = tile_col[0]
    weight = 1.0 / math.sqrt(scen)

    def of_core(zero, one):
        return jnp.where(core == 0, zero, one)

    def send(block, source):
        return lax.ppermute(block, "phase", [(source, 1 - source)])

    def swap(block):
        return lax.ppermute(block, "phase", [(0, 1), (1, 0)])

    my_places = jnp.concatenate([tile_output_block[0], cols])
    other_places = swap(my_places)
    places = [of_core(my_places, other_places), of_core(other_places, my_places)]
    split_rows = []
    for place in places:
        rows = place[: shards * slots].reshape(shards, slots)
        split_rows.append(of_core(rows[:, :half], rows[:, half:]).reshape(-1))
    my_number = core[None].astype(jnp.int32)
    split_meta = jnp.concatenate([my_number, of_core(places[1][-slots:-half], cols[half:])])
    meta = jnp.concatenate([my_number, cols])

    sent = first_products(cols, normals, tiles, half, half)
    kept = first_products(cols, normals, tiles, 0, half)
    outgoing, tiles_now = lax.optimization_barrier((of_core(kept, send(sent, 0)), tiles))
    received = send(tiles_now, 1)
    arrived = exchange(outgoing)
    part = add_up(split_rows[0], arrived, blocks)
    shock_slices = (part + swap(part)).astype(jnp.bfloat16)

    scales = jnp.stack([three_terms(notional), three_terms(strike)])
    scales = scales.reshape(6, blocks_dev, shards, SLICE).transpose(2, 0, 1, 3)
    scales = scales.reshape(shards, 1, 6 * blocks_dev * SLICE).astype(jnp.bfloat16)
    scales = jnp.pad(scales, ((0, 0), (0, SLICE - 1), (0, scen - scales.shape[2])))
    shock_rows = shock_slices.reshape(shards, blocks_dev * SLICE, scen)
    arrived = exchange(jnp.concatenate([shock_rows, scales], axis=1))
    shocks = arrived[:, : blocks_dev * SLICE].reshape(shards, blocks_dev, SLICE, scen)
    shocks = shocks.transpose(1, 0, 2, 3).reshape(blocks_dev, width, scen)
    shocks_natural = shocks.transpose(2, 0, 1).reshape(scen, local_width)
    scales = arrived[:, blocks_dev * SLICE, : 6 * blocks_dev * SLICE].astype(jnp.float32)
    scales = scales.reshape(shards, 2, 3, blocks_dev, SLICE)
    scales = (scales[:, :, 0] + scales[:, :, 1]) + scales[:, :, 2]
    scales = scales.transpose(1, 0, 2, 3).reshape(2, blocks, SLICE, 1)

    arrived = exchange(split_products(split_meta, shocks_natural, received, tiles))
    part = add_up(split_rows[1], arrived, blocks)
    outgoing = value_and_hand_out(
        split_rows[1], part, swap(part), scales[0], scales[1], shards, half, weight
    )

    high1 = exchange(outgoing)
    part = split_backward(split_meta, high1, received, tiles, blocks_dev)
    shock_grad = (part + swap(part)).astype(jnp.bfloat16)
    low1 = send(high1, 0)

    shock_grad = shock_grad.reshape(blocks_dev, shards, SLICE, scen).transpose(1, 0, 2, 3)
    arrived = exchange(shock_grad.reshape(shards, blocks_dev * SLICE, scen))
    low0 = exchange(only_hand_out(split_rows[0], arrived, shards, half))
    high0 = send(low0, 1)

    normals_held = normals.reshape(scen, blocks_dev, width).transpose(1, 2, 0)
    inputs = of_core(normals_held, shocks)
    sens, part = last_backward(meta, low0, low1, inputs, tiles, 0, half)
    sens, adjoint = last_backward(meta, high0, high1, inputs, tiles, half, half, (part, sens))
    return sens[None], adjoint[None]


def solution(mesh):
    return jax.shard_map(
        on_device,
        mesh=mesh,
        in_specs=(
            P(None, "blk"),
            P("phase", "blk", None, None),
            P("phase", None),
            P("phase", "blk"),
            P("blk"),
            P("blk"),
        ),
        out_specs=(P("phase", "blk", None, None), P("phase", None, "blk")),
        check_vma=False,
    )
```

```python
import functools
import math

import jax
import jax.numpy as jnp
from jax import lax
from jax.experimental import pallas as pl
from jax.experimental.pallas import tpu as pltpu
from jax.sharding import PartitionSpec as P

SLICE = 8
VMEM_LIMIT = 16 * 1024 * 1024
STREAM_LIMIT = 48 * 1024 * 1024
PASSING_LIMIT = 45 * 1024 * 1024


def params(limit=VMEM_LIMIT):
    return pltpu.CompilerParams(vmem_limit_bytes=limit)


def tile_copies(source, first, held, sems):
    def copy(k):
        return pltpu.make_async_copy(
            source.at[pl.ds(first + 2 * k, 2)], held.at[pl.ds(2 * k, 2)], sems.at[k]
        )

    return copy


def tile_scratch(count, width):
    return [pltpu.VMEM((count, width, width), jnp.bfloat16), pltpu.SemaphoreType.DMA((count // 2,))]


def product_pair(cols, at, x, tiles, out, pair):
    width = tiles.shape[1]
    parts = []
    for u in range(2):
        col = cols[at + 2 * pair + u]
        picked = x[:, pl.ds(pl.multiple_of(col * width, width), width)]
        product = jnp.dot(picked, tiles[2 * pair + u], preferred_element_type=jnp.float32)
        parts.append(product.T.reshape(width // SLICE, SLICE, x.shape[0]))
    both = jnp.concatenate(parts, axis=1).astype(jnp.bfloat16)
    out[:, 2 * SLICE * pair : 2 * SLICE * (pair + 1), :] = both


def first_products_body(
    cols_in, x_in, tiles, out, *rest, first
):
    *low, cols, x, small_sems, held, sems, low_sems = rest
    pairs = held.shape[0] // 2
    copy = tile_copies(tiles, first, held, sems)
    cols_copy = pltpu.make_async_copy(cols_in, cols, small_sems.at[0])
    x_copy = pltpu.make_async_copy(x_in, x, small_sems.at[1])
    cols_copy.start()
    x_copy.start()
    for k in range(pairs):
        copy(k).start()
    cols_copy.wait()
    x_copy.wait()

    def multiply():
        for k in range(pairs):
            copy(k).wait()
            product_pair(cols.at[0], first, x, held, out, k)

    if not low:
        multiply()
        return
    core = lax.axis_index("phase")
    pl.when(core == 0)(multiply)

    @pl.when(core == 1)
    def _():
        def put(k):
            return pltpu.make_async_copy(
                held.at[pl.ds(2 * k, 2)], low[0].at[pl.ds(2 * k, 2)], low_sems.at[k]
            )

        for k in range(pairs):
            copy(k).wait()
            put(k).start()
        for k in range(pairs):
            put(k).wait()


def first_products(cols, x, tiles, first, count, keep):
    width = tiles.shape[1]
    scen = x.shape[0]
    vmem = pl.BlockSpec(memory_space=pltpu.VMEM)
    hbm = pl.BlockSpec(memory_space=pl.ANY)
    out = jax.ShapeDtypeStruct((width // SLICE, count * SLICE, scen), jnp.bfloat16)
    low = jax.ShapeDtypeStruct((count, width, width), jnp.bfloat16)
    return pl.pallas_call(
        functools.partial(first_products_body, first=first),
        in_specs=[hbm, hbm, hbm],
        out_specs=[vmem, hbm] if keep else vmem,
        out_shape=[out, low] if keep else out,
        scratch_shapes=[
            pltpu.SMEM(cols.shape, jnp.int32),
            pltpu.VMEM(x.shape, jnp.bfloat16),
            pltpu.SemaphoreType.DMA((2,)),
        ]
        + tile_scratch(count, width)
        + [pltpu.SemaphoreType.DMA((count // 2,))],
        compiler_params=params(STREAM_LIMIT),
        name="first_products",
    )(cols, x, tiles)


def start_split_tiles(core, received, tiles, held, sems):
    count = held.shape[0]

    @pl.when(core == 0)
    def _():
        for k in range(count // 2):
            tile_copies(received, 0, held, sems)(k).start()

    @pl.when(core == 1)
    def _():
        for k in range(count // 2):
            tile_copies(tiles, count, held, sems)(k).start()

    return tile_copies(received, 0, held, sems)


def split_products_body(meta, x, received, tiles, out, held, sems, stage, out_sems):
    pairs = held.shape[0] // 2
    copy = start_split_tiles(meta[0], received, tiles, held, sems)

    def put(k):
        rows = slice(2 * SLICE * k, 2 * SLICE * (k + 1))
        return pltpu.make_async_copy(stage.at[:, rows], out.at[:, rows], out_sems.at[k])

    for k in range(pairs):
        copy(k).wait()
        product_pair(meta, 1, x, held, stage, k)
        put(k).start()
    for k in range(pairs):
        put(k).wait()


def split_products(meta, x, received, tiles):
    count, width = received.shape[0], received.shape[1]
    out_shape = (width // SLICE, count * SLICE, x.shape[0])
    vmem = pl.BlockSpec(memory_space=pltpu.VMEM)
    hbm = pl.BlockSpec(memory_space=pl.ANY)
    return pl.pallas_call(
        split_products_body,
        in_specs=[pl.BlockSpec(memory_space=pltpu.SMEM), vmem, hbm, hbm],
        out_specs=hbm,
        out_shape=jax.ShapeDtypeStruct(out_shape, jnp.bfloat16),
        scratch_shapes=tile_scratch(count, width)
        + [pltpu.VMEM(out_shape, jnp.bfloat16), pltpu.SemaphoreType.DMA((count // 2,))],
        compiler_params=params(STREAM_LIMIT),
        name="split_products",
    )(meta, x, received, tiles)


def add_up_body(idx, data, out, second, *, count):
    out[...] = jnp.zeros_like(out)
    second[...] = jnp.zeros_like(second)

    @pl.loop(0, data.shape[0], step=2)
    def _(i):
        for holder, total in ((i, out), (i + 1, second)):
            values = data[holder].astype(jnp.float32)
            places = [idx[holder * count + t] for t in range(count)]
            sums = [
                total[places[t]] + values[t * SLICE : (t + 1) * SLICE] for t in range(count)
            ]
            for t in range(count):
                total[places[t]] = sums[t]

    out[...] += second[...]


def add_up(idx, data, blocks):
    count = data.shape[1] // SLICE
    return pl.pallas_call(
        functools.partial(add_up_body, count=count),
        in_specs=[pl.BlockSpec(memory_space=pltpu.SMEM), pl.BlockSpec(memory_space=pltpu.VMEM)],
        out_specs=pl.BlockSpec(memory_space=pltpu.VMEM),
        out_shape=jax.ShapeDtypeStruct((blocks, SLICE, data.shape[2]), jnp.float32),
        scratch_shapes=[pltpu.VMEM((blocks, SLICE, data.shape[2]), jnp.float32)],
        compiler_params=params(),
        name="add_up",
    )(idx, data)


def hand_out(idx, held, out, count):
    @pl.loop(0, out.shape[0], step=4)
    def _(i):
        for holder in (i, i + 1, i + 2, i + 3):
            for t in range(0, count, 2):
                pair = [held[idx[holder * count + t]], held[idx[holder * count + t + 1]]]
                rows = jnp.concatenate(pair, axis=0).astype(jnp.bfloat16)
                out[holder, t * SLICE : (t + 2) * SLICE, :] = rows


def value_and_hand_out_body(idx, mine, other, notional, strike, out, held, *, count, weight):
    @pl.loop(0, held.shape[0], step=32)
    def _(b):
        for k in range(32):
            moneyness = mine[b + k] + other[b + k]
            held[b + k] = notional[b + k] * jax.nn.sigmoid(moneyness - strike[b + k]) * weight

    hand_out(idx, held, out, count)


def value_and_hand_out(idx, mine, other, notional, strike, shards, count, weight):
    scen = mine.shape[2]
    vmem = pl.BlockSpec(memory_space=pltpu.VMEM)
    return pl.pallas_call(
        functools.partial(value_and_hand_out_body, count=count, weight=weight),
        in_specs=[pl.BlockSpec(memory_space=pltpu.SMEM), vmem, vmem, vmem, vmem],
        out_specs=vmem,
        out_shape=jax.ShapeDtypeStruct((shards, count * SLICE, scen), jnp.bfloat16),
        scratch_shapes=[pltpu.VMEM(mine.shape, jnp.float32)],
        compiler_params=params(),
        name="value_and_hand_out",
    )(idx, mine, other, notional, strike)


def only_hand_out_body(idx, blocks, out, held, *, count):
    held[...] = blocks[...].astype(jnp.float32).reshape(held.shape)
    hand_out(idx, held, out, count)


def only_hand_out(idx, blocks, shards, count):
    scen = blocks.shape[2]
    vmem = pl.BlockSpec(memory_space=pltpu.VMEM)
    held = blocks.shape[0] * blocks.shape[1] // SLICE
    return pl.pallas_call(
        functools.partial(only_hand_out_body, count=count),
        in_specs=[pl.BlockSpec(memory_space=pltpu.SMEM), vmem],
        out_specs=vmem,
        out_shape=jax.ShapeDtypeStruct((shards, count * SLICE, scen), jnp.bfloat16),
        scratch_shapes=[pltpu.VMEM((held, SLICE, scen), jnp.float32)],
        compiler_params=params(),
        name="hand_out",
    )(idx, blocks)


def tile_grad_pair(grads, pair):
    rows = grads[:, 2 * SLICE * pair : 2 * SLICE * (pair + 1), :].astype(jnp.float32)
    width = rows.shape[0] * SLICE
    return [
        rows[:, u * SLICE : (u + 1) * SLICE, :].reshape(width, -1).astype(jnp.bfloat16)
        for u in range(2)
    ]


def split_backward_body(meta, grads, received, tiles, total, held, sems):
    copy = start_split_tiles(meta[0], received, tiles, held, sems)
    total[...] = jnp.zeros_like(total)

    for k in range(held.shape[0] // 2):
        copy(k).wait()
        for u, grad in enumerate(tile_grad_pair(grads, k)):
            product = jnp.dot(held[2 * k + u], grad, preferred_element_type=jnp.float32)
            total[meta[1 + 2 * k + u]] += product


def split_backward(meta, grads, received, tiles, blocks_dev):
    count, width = received.shape[0], received.shape[1]
    vmem = pl.BlockSpec(memory_space=pltpu.VMEM)
    hbm = pl.BlockSpec(memory_space=pl.ANY)
    return pl.pallas_call(
        split_backward_body,
        in_specs=[pl.BlockSpec(memory_space=pltpu.SMEM), vmem, hbm, hbm],
        out_specs=vmem,
        out_shape=jax.ShapeDtypeStruct((blocks_dev, width, grads.shape[2]), jnp.float32),
        scratch_shapes=tile_scratch(count, width),
        compiler_params=params(STREAM_LIMIT),
        name="split_backward",
    )(meta, grads, received, tiles)


def last_backward_body(meta, grads0, grads1, inputs, tiles, *rest, first):
    if first:
        earlier, _, sens, adjoint_out, grads, grads_sems, stage, out_sems, *more = rest
        total, adjoint, adjoint_sem = more
        held = tiles
    else:
        sens, total, following, grads, grads_sems, stage, out_sems, held, sems, next_sems = rest

    pairs = stage.shape[0]

    def grads_copy(source, k):
        rows = slice(2 * SLICE * k, 2 * SLICE * (k + 1))
        return pltpu.make_async_copy(source.at[:, rows], grads.at[:, rows], grads_sems.at[k])

    @pl.when(meta[0] == 0)
    def _():
        for k in range(pairs):
            grads_copy(grads0, k).start()

    @pl.when(meta[0] == 1)
    def _():
        for k in range(pairs):
            grads_copy(grads1, k).start()

    if not first:
        take = tile_copies(tiles, 0, held, sems)
        take_next = tile_copies(tiles, held.shape[0], following, next_sems)
        for k in range(held.shape[0] // 2):
            take(k).start()
        for k in range(held.shape[0] // 2):
            take_next(k).start()

    total[...] = earlier[...] if first else jnp.zeros_like(total)

    def put(k):
        return pltpu.make_async_copy(
            stage.at[k // 2, k % 2], sens.at[first + k], out_sems.at[k]
        )

    for k in range(pairs):
        if not first:
            take(k).wait()
        grads_copy(grads0, k).wait()
        for u, grad in enumerate(tile_grad_pair(grads, k)):
            col = meta[1 + first + 2 * k + u]
            total[col] += jnp.dot(held[2 * k + u], grad, preferred_element_type=jnp.float32)
            stage[k, u] = lax.dot_general(
                inputs[col], grad, (((1,), (1,)), ((), ())), preferred_element_type=jnp.float32
            ).astype(jnp.bfloat16)
            put(2 * k + u).start()

    if first:
        width = total.shape[1]
        for c in range(total.shape[0]):
            adjoint[:, c * width : (c + 1) * width] = total[c].T.astype(jnp.bfloat16)
        adjoint_copy = pltpu.make_async_copy(adjoint, adjoint_out, adjoint_sem)
        adjoint_copy.start()
        adjoint_copy.wait()
    else:
        for k in range(pairs):
            take_next(k).wait()
    for k in range(2 * pairs):
        put(k).wait()


def last_backward_calls(meta, grads, inputs, tiles):
    slots, width, _ = tiles.shape
    half = slots // 2
    blocks_dev, _, scen = inputs.shape
    smem = pl.BlockSpec(memory_space=pltpu.SMEM)
    vmem = pl.BlockSpec(memory_space=pltpu.VMEM)
    hbm = pl.BlockSpec(memory_space=pl.ANY)
    sens_shape = jax.ShapeDtypeStruct((slots, width, width), jnp.bfloat16)
    total_shape = jax.ShapeDtypeStruct(inputs.shape, jnp.float32)
    half_shape = jax.ShapeDtypeStruct((half, width, width), jnp.bfloat16)
    sems = pltpu.SemaphoreType.DMA((half // 2,))
    scratch = [
        pltpu.VMEM(grads[0][0].shape, jnp.bfloat16),
        sems,
        pltpu.VMEM((half // 2, 2, width, width), jnp.bfloat16),
        pltpu.SemaphoreType.DMA((half,)),
    ]
    adjoint_shape = (scen, blocks_dev * width)
    sens, total, high_tiles = pl.pallas_call(
        functools.partial(last_backward_body, first=0),
        in_specs=[smem, hbm, hbm, vmem, hbm],
        out_specs=[hbm, vmem, vmem],
        out_shape=[sens_shape, total_shape, half_shape],
        scratch_shapes=[*scratch, *tile_scratch(half, width), sems],
        compiler_params=params(PASSING_LIMIT),
        name="last_backward_low",
    )(meta, *grads[0], inputs, tiles)
    return pl.pallas_call(
        functools.partial(last_backward_body, first=half),
        in_specs=[smem, hbm, hbm, vmem, vmem, vmem, hbm],
        out_specs=[hbm, hbm],
        out_shape=[sens_shape, jax.ShapeDtypeStruct(adjoint_shape, jnp.bfloat16)],
        scratch_shapes=[
            *scratch,
            pltpu.VMEM(inputs.shape, jnp.float32),
            pltpu.VMEM(adjoint_shape, jnp.bfloat16),
            pltpu.SemaphoreType.DMA,
        ],
        input_output_aliases={6: 0},
        compiler_params=params(),
        name="last_backward_high",
    )(meta, *grads[1], inputs, high_tiles, total, sens)


def three_terms(values):
    terms = []
    for _ in range(3):
        term = lax.reduce_precision(values, 8, 7)
        terms.append(term)
        values = values - term
    return jnp.stack(terms)


def exchange(block):
    return lax.all_to_all(block, "blk", split_axis=0, concat_axis=0, tiled=True)


def on_device(normals, section_tile_list, tile_output_block, tile_col, notional, strike):
    shards = lax.axis_size("blk")
    core = lax.axis_index("phase")
    tiles = section_tile_list[0]
    slots, width, _ = tiles.shape
    half = slots // 2
    scen, local_width = normals.shape
    blocks_dev = local_width // width
    blocks = shards * blocks_dev
    cols = tile_col[0]
    weight = 1.0 / math.sqrt(scen)

    def of_core(zero, one):
        return jnp.where(core == 0, zero, one)

    def send(block, source):
        return lax.ppermute(block, "phase", [(source, 1 - source)])

    def swap(block):
        return lax.ppermute(block, "phase", [(0, 1), (1, 0)])

    my_places = jnp.concatenate([tile_output_block[0], cols])
    other_places = swap(my_places)
    places = [of_core(my_places, other_places), of_core(other_places, my_places)]
    split_rows = []
    for place in places:
        rows = place[: shards * slots].reshape(shards, slots)
        split_rows.append(of_core(rows[:, :half], rows[:, half:]).reshape(-1))
    my_number = core[None].astype(jnp.int32)
    split_meta = jnp.concatenate([my_number, of_core(places[1][-slots:-half], cols[half:])])
    meta = jnp.concatenate([my_number, cols])

    sent = first_products(tile_col, normals, tiles, half, half, False)
    kept, low_tiles = first_products(tile_col, normals, tiles, 0, half, True)
    arrived = exchange(of_core(kept, send(sent, 0)))
    part = add_up(split_rows[0], arrived, blocks)
    other_part, low_tiles = lax.optimization_barrier((swap(part), low_tiles))
    received = send(low_tiles, 1)
    shock_slices = (part + other_part).astype(jnp.bfloat16)

    scales = jnp.stack([three_terms(notional), three_terms(strike)])
    scales = scales.reshape(6, blocks_dev, shards, SLICE).transpose(2, 0, 1, 3)
    scales = scales.reshape(shards, 1, 6 * blocks_dev * SLICE).astype(jnp.bfloat16)
    scales = jnp.pad(scales, ((0, 0), (0, SLICE - 1), (0, scen - scales.shape[2])))
    shock_rows = shock_slices.reshape(shards, blocks_dev * SLICE, scen)
    arrived = exchange(jnp.concatenate([shock_rows, scales], axis=1))
    shocks = arrived[:, : blocks_dev * SLICE].reshape(shards, blocks_dev, SLICE, scen)
    shocks = shocks.transpose(1, 0, 2, 3).reshape(blocks_dev, width, scen)
    shocks_natural = shocks.transpose(2, 0, 1).reshape(scen, local_width)
    scales = arrived[:, blocks_dev * SLICE, : 6 * blocks_dev * SLICE].astype(jnp.float32)
    scales = scales.reshape(shards, 2, 3, blocks_dev, SLICE)
    scales = (scales[:, :, 0] + scales[:, :, 1]) + scales[:, :, 2]
    scales = scales.transpose(1, 0, 2, 3).reshape(2, blocks, SLICE, 1)

    arrived = exchange(split_products(split_meta, shocks_natural, received, tiles))
    part = add_up(split_rows[1], arrived, blocks)
    outgoing = value_and_hand_out(
        split_rows[1], part, swap(part), scales[0], scales[1], shards, half, weight
    )

    high1 = exchange(outgoing)
    part = split_backward(split_meta, high1, received, tiles, blocks_dev)
    shock_grad = (part + swap(part)).astype(jnp.bfloat16)
    low1 = send(high1, 0)

    shock_grad = shock_grad.reshape(blocks_dev, shards, SLICE, scen).transpose(1, 0, 2, 3)
    arrived = exchange(shock_grad.reshape(shards, blocks_dev * SLICE, scen))
    low0 = exchange(only_hand_out(split_rows[0], arrived, shards, half))
    high0 = send(low0, 1)

    normals_held = normals.reshape(scen, blocks_dev, width).transpose(1, 2, 0)
    inputs = of_core(normals_held, shocks)
    sens, adjoint = last_backward_calls(
        meta, ((low0, low1), (high0, high1)), inputs, tiles
    )
    return sens[None], adjoint[None]


def solution(mesh):
    return jax.shard_map(
        on_device,
        mesh=mesh,
        in_specs=(
            P(None, "blk"),
            P("phase", "blk", None, None),
            P("phase", None),
            P("phase", "blk"),
            P("blk"),
            P("blk"),
        ),
        out_specs=(P("phase", "blk", None, None), P("phase", None, "blk")),
        check_vma=False,
    )
```

```python
import functools
import math

import jax
import jax.numpy as jnp
from jax import lax
from jax.experimental import pallas as pl
from jax.experimental.pallas import tpu as pltpu
from jax.sharding import PartitionSpec as P

SLICE = 8
VMEM_LIMIT = 16 * 1024 * 1024
STREAM_LIMIT = 48 * 1024 * 1024
PASSING_LIMIT = 45 * 1024 * 1024


def params(limit=VMEM_LIMIT):
    return pltpu.CompilerParams(vmem_limit_bytes=limit)


def tile_copies(source, first, held, sems):
    def copy(k):
        return pltpu.make_async_copy(
            source.at[pl.ds(first + 2 * k, 2)], held.at[pl.ds(2 * k, 2)], sems.at[k]
        )

    return copy


def tile_scratch(count, width):
    return [pltpu.VMEM((count, width, width), jnp.bfloat16), pltpu.SemaphoreType.DMA((count // 2,))]


def product_pair(cols, at, x, tiles, out, pair):
    width = tiles.shape[1]
    parts = []
    for u in range(2):
        col = cols[at + 2 * pair + u]
        picked = x[:, pl.ds(pl.multiple_of(col * width, width), width)]
        product = jnp.dot(picked, tiles[2 * pair + u], preferred_element_type=jnp.float32)
        parts.append(product.T.reshape(width // SLICE, SLICE, x.shape[0]))
    both = jnp.concatenate(parts, axis=1).astype(jnp.bfloat16)
    out[:, 2 * SLICE * pair : 2 * SLICE * (pair + 1), :] = both


def put_rows(stage, out, sems, k):
    rows = slice(2 * SLICE * k, 2 * SLICE * (k + 1))
    return pltpu.make_async_copy(stage.at[:, rows], out.at[:, rows], sems.at[k])


def first_products_body(
    cols_in, x_in, tiles, out, *rest, first
):
    *low, cols, x, small_sems, held, sems, low_sems = rest
    pairs = held.shape[0] // 2
    copy = tile_copies(tiles, first, held, sems)
    cols_copy = pltpu.make_async_copy(cols_in, cols, small_sems.at[0])
    x_copy = pltpu.make_async_copy(x_in, x, small_sems.at[1])
    cols_copy.start()
    x_copy.start()
    for k in range(pairs):
        copy(k).start()
    cols_copy.wait()
    x_copy.wait()

    def multiply():
        for k in range(pairs):
            copy(k).wait()
            product_pair(cols.at[0], first, x, held, out, k)

    if not low:
        multiply()
        return
    core = lax.axis_index("phase")
    pl.when(core == 0)(multiply)

    @pl.when(core == 1)
    def _():
        def put(k):
            return pltpu.make_async_copy(
                held.at[pl.ds(2 * k, 2)], low[0].at[pl.ds(2 * k, 2)], low_sems.at[k]
            )

        for k in range(pairs):
            copy(k).wait()
            put(k).start()
        for k in range(pairs):
            put(k).wait()


def first_products(cols, x, tiles, first, count, keep):
    width = tiles.shape[1]
    scen = x.shape[0]
    vmem = pl.BlockSpec(memory_space=pltpu.VMEM)
    hbm = pl.BlockSpec(memory_space=pl.ANY)
    out = jax.ShapeDtypeStruct((width // SLICE, count * SLICE, scen), jnp.bfloat16)
    low = jax.ShapeDtypeStruct((count, width, width), jnp.bfloat16)
    return pl.pallas_call(
        functools.partial(first_products_body, first=first),
        in_specs=[hbm, hbm, hbm],
        out_specs=[vmem, hbm] if keep else vmem,
        out_shape=[out, low] if keep else out,
        scratch_shapes=[
            pltpu.SMEM(cols.shape, jnp.int32),
            pltpu.VMEM(x.shape, jnp.bfloat16),
            pltpu.SemaphoreType.DMA((2,)),
        ]
        + tile_scratch(count, width)
        + [pltpu.SemaphoreType.DMA((count // 2,))],
        compiler_params=params(STREAM_LIMIT),
        name="first_products",
    )(cols, x, tiles)


def start_split_tiles(core, received, tiles, held, sems):
    count = held.shape[0]

    @pl.when(core == 0)
    def _():
        for k in range(count // 2):
            tile_copies(received, 0, held, sems)(k).start()

    @pl.when(core == 1)
    def _():
        for k in range(count // 2):
            tile_copies(tiles, count, held, sems)(k).start()

    return tile_copies(received, 0, held, sems)


def split_products_body(meta, x, received, tiles, out, held, sems, stage, out_sems):
    pairs = held.shape[0] // 2
    copy = start_split_tiles(meta[0], received, tiles, held, sems)

    for k in range(pairs):
        copy(k).wait()
        product_pair(meta, 1, x, held, stage, k)
        put_rows(stage, out, out_sems, k).start()
    for k in range(pairs):
        put_rows(stage, out, out_sems, k).wait()


def split_products(meta, x, received, tiles):
    count, width = received.shape[0], received.shape[1]
    out_shape = (width // SLICE, count * SLICE, x.shape[0])
    vmem = pl.BlockSpec(memory_space=pltpu.VMEM)
    hbm = pl.BlockSpec(memory_space=pl.ANY)
    return pl.pallas_call(
        split_products_body,
        in_specs=[pl.BlockSpec(memory_space=pltpu.SMEM), vmem, hbm, hbm],
        out_specs=hbm,
        out_shape=jax.ShapeDtypeStruct(out_shape, jnp.bfloat16),
        scratch_shapes=tile_scratch(count, width)
        + [pltpu.VMEM(out_shape, jnp.bfloat16), pltpu.SemaphoreType.DMA((count // 2,))],
        compiler_params=params(STREAM_LIMIT),
        name="split_products",
    )(meta, x, received, tiles)


def add_up_body(idx, data, out, second, *, count):
    out[...] = jnp.zeros_like(out)
    second[...] = jnp.zeros_like(second)

    @pl.loop(0, data.shape[0], step=2)
    def _(i):
        for holder, total in ((i, out), (i + 1, second)):
            values = data[holder].astype(jnp.float32)
            places = [idx[holder * count + t] for t in range(count)]
            sums = [
                total[places[t]] + values[t * SLICE : (t + 1) * SLICE] for t in range(count)
            ]
            for t in range(count):
                total[places[t]] = sums[t]

    out[...] += second[...]


def add_up(idx, data, blocks):
    count = data.shape[1] // SLICE
    return pl.pallas_call(
        functools.partial(add_up_body, count=count),
        in_specs=[pl.BlockSpec(memory_space=pltpu.SMEM), pl.BlockSpec(memory_space=pltpu.VMEM)],
        out_specs=pl.BlockSpec(memory_space=pltpu.VMEM),
        out_shape=jax.ShapeDtypeStruct((blocks, SLICE, data.shape[2]), jnp.float32),
        scratch_shapes=[pltpu.VMEM((blocks, SLICE, data.shape[2]), jnp.float32)],
        compiler_params=params(),
        name="add_up",
    )(idx, data)


def hand_out(idx, held, out, count):
    @pl.loop(0, out.shape[0], step=4)
    def _(i):
        for holder in (i, i + 1, i + 2, i + 3):
            for t in range(0, count, 2):
                pair = [held[idx[holder * count + t]], held[idx[holder * count + t + 1]]]
                rows = jnp.concatenate(pair, axis=0).astype(jnp.bfloat16)
                out[holder, t * SLICE : (t + 2) * SLICE, :] = rows


def value_and_hand_out_body(
    idx, mine, other, notional, strike, received, tiles, out, taken, held, sem, *, count, weight
):
    core = lax.axis_index("phase")
    half = taken.shape[0]

    @pl.when(core == 0)
    def _():
        pltpu.make_async_copy(received, taken, sem).start()

    @pl.when(core == 1)
    def _():
        pltpu.make_async_copy(tiles.at[pl.ds(half, half)], taken, sem).start()

    @pl.loop(0, held.shape[0], step=32)
    def _(b):
        for k in range(32):
            moneyness = mine[b + k] + other[b + k]
            held[b + k] = notional[b + k] * jax.nn.sigmoid(moneyness - strike[b + k]) * weight

    hand_out(idx, held, out, count)
    pltpu.make_async_copy(received, taken, sem).wait()


def value_and_hand_out(
    idx, mine, other, notional, strike, received, tiles, shards, count, weight
):
    scen = mine.shape[2]
    vmem = pl.BlockSpec(memory_space=pltpu.VMEM)
    hbm = pl.BlockSpec(memory_space=pl.ANY)
    return pl.pallas_call(
        functools.partial(value_and_hand_out_body, count=count, weight=weight),
        in_specs=[pl.BlockSpec(memory_space=pltpu.SMEM), vmem, vmem, vmem, vmem, hbm, hbm],
        out_specs=[vmem, vmem],
        out_shape=[
            jax.ShapeDtypeStruct((shards, count * SLICE, scen), jnp.bfloat16),
            jax.ShapeDtypeStruct(received.shape, jnp.bfloat16),
        ],
        scratch_shapes=[pltpu.VMEM(mine.shape, jnp.float32), pltpu.SemaphoreType.DMA],
        compiler_params=params(PASSING_LIMIT),
        name="value_and_hand_out",
    )(idx, mine, other, notional, strike, received, tiles)


def only_hand_out_body(idx, blocks, out, held, *, count):
    held[...] = blocks[...].astype(jnp.float32).reshape(held.shape)
    hand_out(idx, held, out, count)


def only_hand_out(idx, blocks, shards, count):
    scen = blocks.shape[2]
    vmem = pl.BlockSpec(memory_space=pltpu.VMEM)
    held = blocks.shape[0] * blocks.shape[1] // SLICE
    return pl.pallas_call(
        functools.partial(only_hand_out_body, count=count),
        in_specs=[pl.BlockSpec(memory_space=pltpu.SMEM), vmem],
        out_specs=vmem,
        out_shape=jax.ShapeDtypeStruct((shards, count * SLICE, scen), jnp.bfloat16),
        scratch_shapes=[pltpu.VMEM((held, SLICE, scen), jnp.float32)],
        compiler_params=params(),
        name="hand_out",
    )(idx, blocks)


def tile_grad_pair(grads, pair):
    rows = grads[:, 2 * SLICE * pair : 2 * SLICE * (pair + 1), :].astype(jnp.float32)
    width = rows.shape[0] * SLICE
    return [
        rows[:, u * SLICE : (u + 1) * SLICE, :].reshape(width, -1).astype(jnp.bfloat16)
        for u in range(2)
    ]


def first_backward_body(meta, grads, tiles, total):
    total[...] = jnp.zeros_like(total)
    for k in range(tiles.shape[0] // 2):
        for u, grad in enumerate(tile_grad_pair(grads, k)):
            product = jnp.dot(tiles[2 * k + u], grad, preferred_element_type=jnp.float32)
            total[meta[1 + 2 * k + u]] += product


def first_backward(meta, grads, tiles, blocks_dev):
    vmem = pl.BlockSpec(memory_space=pltpu.VMEM)
    return pl.pallas_call(
        first_backward_body,
        in_specs=[pl.BlockSpec(memory_space=pltpu.SMEM), vmem, vmem],
        out_specs=vmem,
        out_shape=jax.ShapeDtypeStruct(
            (blocks_dev, tiles.shape[1], grads.shape[2]), jnp.float32
        ),
        compiler_params=params(),
        name="first_backward",
    )(meta, grads, tiles)


def last_backward_body(meta, grads0, grads1, inputs, tiles, *rest, first):
    if first:
        earlier, _, sens, adjoint_out, *scratch, total, adjoint, adjoint_sem = rest
    else:
        sens, total, *scratch = rest
    grads, grads_sems, stage, out_sems, held, sems = scratch
    take = tile_copies(tiles, first, held, sems)

    pairs = stage.shape[0]

    def grads_copy(source, k):
        rows = slice(2 * SLICE * k, 2 * SLICE * (k + 1))
        return pltpu.make_async_copy(source.at[:, rows], grads.at[:, rows], grads_sems.at[k])

    @pl.when(meta[0] == 0)
    def _():
        for k in range(pairs):
            grads_copy(grads0, k).start()

    @pl.when(meta[0] == 1)
    def _():
        for k in range(pairs):
            grads_copy(grads1, k).start()

    for k in range(pairs):
        take(k).start()
    total[...] = earlier[...] if first else jnp.zeros_like(total)

    def put(k):
        return pltpu.make_async_copy(
            stage.at[k // 2, k % 2], sens.at[first + k], out_sems.at[k]
        )

    for k in range(pairs):
        take(k).wait()
        grads_copy(grads0, k).wait()
        for u, grad in enumerate(tile_grad_pair(grads, k)):
            col = meta[1 + first + 2 * k + u]
            total[col] += jnp.dot(held[2 * k + u], grad, preferred_element_type=jnp.float32)
            stage[k, u] = lax.dot_general(
                inputs[col], grad, (((1,), (1,)), ((), ())), preferred_element_type=jnp.float32
            ).astype(jnp.bfloat16)
            put(2 * k + u).start()

    if first:
        width = total.shape[1]
        for c in range(total.shape[0]):
            adjoint[:, c * width : (c + 1) * width] = total[c].T.astype(jnp.bfloat16)
        adjoint_copy = pltpu.make_async_copy(adjoint, adjoint_out, adjoint_sem)
        adjoint_copy.start()
        adjoint_copy.wait()
    for k in range(2 * pairs):
        put(k).wait()


def last_backward_calls(meta, grads, inputs, tiles):
    slots, width, _ = tiles.shape
    half = slots // 2
    blocks_dev, _, scen = inputs.shape
    smem = pl.BlockSpec(memory_space=pltpu.SMEM)
    vmem = pl.BlockSpec(memory_space=pltpu.VMEM)
    hbm = pl.BlockSpec(memory_space=pl.ANY)
    sens_shape = jax.ShapeDtypeStruct((slots, width, width), jnp.bfloat16)
    total_shape = jax.ShapeDtypeStruct(inputs.shape, jnp.float32)
    sems = pltpu.SemaphoreType.DMA((half // 2,))
    scratch = [
        pltpu.VMEM(grads[0][0].shape, jnp.bfloat16),
        sems,
        pltpu.VMEM((half // 2, 2, width, width), jnp.bfloat16),
        pltpu.SemaphoreType.DMA((half,)),
        *tile_scratch(half, width),
    ]
    adjoint_shape = (scen, blocks_dev * width)
    sens, total = pl.pallas_call(
        functools.partial(last_backward_body, first=0),
        in_specs=[smem, hbm, hbm, vmem, hbm],
        out_specs=[hbm, vmem],
        out_shape=[sens_shape, total_shape],
        scratch_shapes=scratch,
        compiler_params=params(STREAM_LIMIT),
        name="last_backward_low",
    )(meta, *grads[0], inputs, tiles)
    return pl.pallas_call(
        functools.partial(last_backward_body, first=half),
        in_specs=[smem, hbm, hbm, vmem, hbm, vmem, hbm],
        out_specs=[hbm, hbm],
        out_shape=[sens_shape, jax.ShapeDtypeStruct(adjoint_shape, jnp.bfloat16)],
        scratch_shapes=[
            *scratch,
            pltpu.VMEM(inputs.shape, jnp.float32),
            pltpu.VMEM(adjoint_shape, jnp.bfloat16),
            pltpu.SemaphoreType.DMA,
        ],
        input_output_aliases={6: 0},
        compiler_params=params(STREAM_LIMIT),
        name="last_backward_high",
    )(meta, *grads[1], inputs, tiles, total, sens)


def three_terms(values):
    terms = []
    for _ in range(3):
        term = lax.reduce_precision(values, 8, 7)
        terms.append(term)
        values = values - term
    return jnp.stack(terms)


def scales_to_send(notional, strike, shards, blocks_dev, scen):
    scales = jnp.stack([three_terms(notional), three_terms(strike)])
    scales = scales.reshape(6, blocks_dev, shards, SLICE).transpose(2, 0, 1, 3)
    scales = scales.reshape(shards, 1, 6 * blocks_dev * SLICE).astype(jnp.bfloat16)
    return jnp.pad(scales, ((0, 0), (0, SLICE - 1), (0, scen - scales.shape[2])))


def exchange(block):
    return lax.all_to_all(block, "blk", split_axis=0, concat_axis=0, tiled=True)


def on_device(normals, section_tile_list, tile_output_block, tile_col, notional, strike):
    shards = lax.axis_size("blk")
    core = lax.axis_index("phase")
    tiles = section_tile_list[0]
    slots, width, _ = tiles.shape
    half = slots // 2
    scen, local_width = normals.shape
    blocks_dev = local_width // width
    blocks = shards * blocks_dev
    cols = tile_col[0]
    weight = 1.0 / math.sqrt(scen)

    def of_core(zero, one):
        return jnp.where(core == 0, zero, one)

    def send(block, source):
        return lax.ppermute(block, "phase", [(source, 1 - source)])

    def swap(block):
        return lax.ppermute(block, "phase", [(0, 1), (1, 0)])

    my_places = jnp.concatenate([tile_output_block[0], cols])
    other_places = swap(my_places)
    places = [of_core(my_places, other_places), of_core(other_places, my_places)]
    split_rows = []
    for place in places:
        rows = place[: shards * slots].reshape(shards, slots)
        split_rows.append(of_core(rows[:, :half], rows[:, half:]).reshape(-1))
    my_number = core[None].astype(jnp.int32)
    split_meta = jnp.concatenate([my_number, of_core(places[1][-slots:-half], cols[half:])])
    meta = jnp.concatenate([my_number, cols])

    sent = first_products(tile_col, normals, tiles, half, half, False)
    kept, low_tiles = first_products(tile_col, normals, tiles, 0, half, True)
    arrived = exchange(of_core(kept, send(sent, 0)))
    scales = scales_to_send(notional, strike, shards, blocks_dev, scen)
    split_rows[0], scales = lax.optimization_barrier((split_rows[0], scales))
    part = add_up(split_rows[0], arrived, blocks)
    other_part, low_tiles = lax.optimization_barrier((swap(part), low_tiles))
    received = send(low_tiles, 1)
    shock_slices = (part + other_part).astype(jnp.bfloat16)

    shock_rows = shock_slices.reshape(shards, blocks_dev * SLICE, scen)
    arrived = exchange(jnp.concatenate([shock_rows, scales], axis=1))
    shocks = arrived[:, : blocks_dev * SLICE].reshape(shards, blocks_dev, SLICE, scen)
    shocks = shocks.transpose(1, 0, 2, 3).reshape(blocks_dev, width, scen)
    shocks_natural = shocks.transpose(2, 0, 1).reshape(scen, local_width)
    scales = arrived[:, blocks_dev * SLICE, : 6 * blocks_dev * SLICE].astype(jnp.float32)
    scales = scales.reshape(shards, 2, 3, blocks_dev, SLICE)
    scales = (scales[:, :, 0] + scales[:, :, 1]) + scales[:, :, 2]
    scales = scales.transpose(1, 0, 2, 3).reshape(2, blocks, SLICE, 1)

    arrived = exchange(split_products(split_meta, shocks_natural, received, tiles))
    split_rows[1], scales = lax.optimization_barrier((split_rows[1], scales))
    part = add_up(split_rows[1], arrived, blocks)
    outgoing, split_tiles = value_and_hand_out(
        split_rows[1],
        part,
        swap(part),
        scales[0],
        scales[1],
        received,
        tiles,
        shards,
        half,
        weight,
    )

    high1 = exchange(outgoing)
    part = first_backward(split_meta, high1, split_tiles, blocks_dev)
    shock_grad = (part + swap(part)).astype(jnp.bfloat16)
    low1 = send(high1, 0)

    shock_grad = shock_grad.reshape(blocks_dev, shards, SLICE, scen).transpose(1, 0, 2, 3)
    arrived = exchange(shock_grad.reshape(shards, blocks_dev * SLICE, scen))
    normals_held = normals.reshape(scen, blocks_dev, width).transpose(1, 2, 0)
    inputs = of_core(normals_held, shocks)
    low0 = exchange(only_hand_out(split_rows[0], arrived, shards, half))
    high0 = send(low0, 1)
    sens, adjoint = last_backward_calls(
        meta, ((low0, low1), (high0, high1)), inputs, tiles
    )
    return sens[None], adjoint[None]


def solution(mesh):
    return jax.shard_map(
        on_device,
        mesh=mesh,
        in_specs=(
            P(None, "blk"),
            P("phase", "blk", None, None),
            P("phase", None),
            P("phase", "blk"),
            P("blk"),
            P("blk"),
        ),
        out_specs=(P("phase", "blk", None, None), P("phase", None, "blk")),
        check_vma=False,
    )
```

```python
import functools
import math

import jax
import jax.numpy as jnp
from jax import lax
from jax.experimental import pallas as pl
from jax.experimental.pallas import tpu as pltpu
from jax.sharding import PartitionSpec as P

SLICE = 8
VMEM_LIMIT = 16 * 1024 * 1024
STREAM_LIMIT = 48 * 1024 * 1024
PASSING_LIMIT = 45 * 1024 * 1024


def params(limit=VMEM_LIMIT):
    return pltpu.CompilerParams(vmem_limit_bytes=limit)


def tile_copies(source, first, held, sems):
    def copy(k):
        return pltpu.make_async_copy(
            source.at[pl.ds(first + 2 * k, 2)], held.at[pl.ds(2 * k, 2)], sems.at[k]
        )

    return copy


def tile_scratch(count, width):
    return [pltpu.VMEM((count, width, width), jnp.bfloat16), pltpu.SemaphoreType.DMA((count // 2,))]


def product_pair(cols, at, x, tiles, out, pair):
    width = tiles.shape[1]
    parts = []
    for u in range(2):
        col = cols[at + 2 * pair + u]
        picked = x[:, pl.ds(pl.multiple_of(col * width, width), width)]
        product = jnp.dot(picked, tiles[2 * pair + u], preferred_element_type=jnp.float32)
        parts.append(product.T.reshape(width // SLICE, SLICE, x.shape[0]))
    both = jnp.concatenate(parts, axis=1).astype(jnp.bfloat16)
    out[:, 2 * SLICE * pair : 2 * SLICE * (pair + 1), :] = both


def put_rows(stage, out, sems, k):
    rows = slice(2 * SLICE * k, 2 * SLICE * (k + 1))
    return pltpu.make_async_copy(stage.at[:, rows], out.at[:, rows], sems.at[k])


def first_products_body(cols_in, x_in, tiles, *rest, first, moved):
    out, low, cols, x, small_sems, held, sems, low_sems = rest[-8:]
    pairs = held.shape[0] // 2
    core = lax.axis_index("phase")

    @pl.when(core == 0)
    def _():
        copy = tile_copies(tiles, first, held, sems)
        cols_copy = pltpu.make_async_copy(cols_in, cols, small_sems.at[0])
        x_copy = pltpu.make_async_copy(x_in, x, small_sems.at[1])
        cols_copy.start()
        x_copy.start()
        for k in range(pairs):
            copy(k).start()
        cols_copy.wait()
        x_copy.wait()
        for k in range(pairs):
            copy(k).wait()
            product_pair(cols.at[0], first, x, held, out, k)

    @pl.when(core == 1)
    def _():
        copy = tile_copies(tiles, 0, held, sems)

        def put(k):
            return pltpu.make_async_copy(
                held.at[pl.ds(2 * k, 2)], low.at[pl.ds(2 * k, 2)], low_sems.at[k]
            )

        for k in moved:
            copy(k).start()
        for k in moved:
            copy(k).wait()
            put(k).start()
        for k in moved:
            put(k).wait()


def first_products(cols, x, tiles, first, count, moved, low=()):
    width = tiles.shape[1]
    scen = x.shape[0]
    vmem = pl.BlockSpec(memory_space=pltpu.VMEM)
    hbm = pl.BlockSpec(memory_space=pl.ANY)
    return pl.pallas_call(
        functools.partial(first_products_body, first=first, moved=moved),
        in_specs=[hbm] * (3 + len(low)),
        out_specs=[vmem, hbm],
        out_shape=[
            jax.ShapeDtypeStruct((width // SLICE, count * SLICE, scen), jnp.bfloat16),
            jax.ShapeDtypeStruct((count, width, width), jnp.bfloat16),
        ],
        scratch_shapes=[
            pltpu.SMEM(cols.shape, jnp.int32),
            pltpu.VMEM(x.shape, jnp.bfloat16),
            pltpu.SemaphoreType.DMA((2,)),
        ]
        + tile_scratch(count, width)
        + [pltpu.SemaphoreType.DMA((count // 2,))],
        input_output_aliases={3: 1} if low else {},
        compiler_params=params(STREAM_LIMIT),
        name="first_products",
    )(cols, x, tiles, *low)


def start_split_tiles(core, received, tiles, held, sems):
    count = held.shape[0]

    @pl.when(core == 0)
    def _():
        for k in range(count // 2):
            tile_copies(received, 0, held, sems)(k).start()

    @pl.when(core == 1)
    def _():
        for k in range(count // 2):
            tile_copies(tiles, count, held, sems)(k).start()

    return tile_copies(received, 0, held, sems)


def split_products_body(meta, x, received, tiles, out, held, sems, stage, out_sems):
    pairs = held.shape[0] // 2
    copy = start_split_tiles(meta[0], received, tiles, held, sems)

    for k in range(pairs):
        copy(k).wait()
        product_pair(meta, 1, x, held, stage, k)
        put_rows(stage, out, out_sems, k).start()
    for k in range(pairs):
        put_rows(stage, out, out_sems, k).wait()


def split_products(meta, x, received, tiles):
    count, width = received.shape[0], received.shape[1]
    out_shape = (width // SLICE, count * SLICE, x.shape[0])
    vmem = pl.BlockSpec(memory_space=pltpu.VMEM)
    hbm = pl.BlockSpec(memory_space=pl.ANY)
    return pl.pallas_call(
        split_products_body,
        in_specs=[pl.BlockSpec(memory_space=pltpu.SMEM), vmem, hbm, hbm],
        out_specs=hbm,
        out_shape=jax.ShapeDtypeStruct(out_shape, jnp.bfloat16),
        scratch_shapes=tile_scratch(count, width)
        + [pltpu.VMEM(out_shape, jnp.bfloat16), pltpu.SemaphoreType.DMA((count // 2,))],
        compiler_params=params(STREAM_LIMIT),
        name="split_products",
    )(meta, x, received, tiles)


def add_up_body(idx, data, out, second, *, count):
    out[...] = jnp.zeros_like(out)
    second[...] = jnp.zeros_like(second)

    @pl.loop(0, data.shape[0], step=2)
    def _(i):
        for holder, total in ((i, out), (i + 1, second)):
            values = data[holder].astype(jnp.float32)
            places = [idx[holder * count + t] for t in range(count)]
            sums = [
                total[places[t]] + values[t * SLICE : (t + 1) * SLICE] for t in range(count)
            ]
            for t in range(count):
                total[places[t]] = sums[t]

    out[...] += second[...]


def add_up(idx, data, blocks):
    count = data.shape[1] // SLICE
    return pl.pallas_call(
        functools.partial(add_up_body, count=count),
        in_specs=[pl.BlockSpec(memory_space=pltpu.SMEM), pl.BlockSpec(memory_space=pltpu.VMEM)],
        out_specs=pl.BlockSpec(memory_space=pltpu.VMEM),
        out_shape=jax.ShapeDtypeStruct((blocks, SLICE, data.shape[2]), jnp.float32),
        scratch_shapes=[pltpu.VMEM((blocks, SLICE, data.shape[2]), jnp.float32)],
        compiler_params=params(),
        name="add_up",
    )(idx, data)


def hand_out(idx, held, out, count):
    @pl.loop(0, out.shape[0], step=4)
    def _(i):
        for holder in (i, i + 1, i + 2, i + 3):
            for t in range(0, count, 2):
                pair = [held[idx[holder * count + t]], held[idx[holder * count + t + 1]]]
                rows = jnp.concatenate(pair, axis=0).astype(jnp.bfloat16)
                out[holder, t * SLICE : (t + 2) * SLICE, :] = rows


def value_and_hand_out_body(
    idx, mine, other, notional, strike, received, tiles, out, taken, held, sem, *, count, weight
):
    core = lax.axis_index("phase")
    half = taken.shape[0]

    @pl.when(core == 0)
    def _():
        pltpu.make_async_copy(received, taken, sem).start()

    @pl.when(core == 1)
    def _():
        pltpu.make_async_copy(tiles.at[pl.ds(half, half)], taken, sem).start()

    @pl.loop(0, held.shape[0], step=32)
    def _(b):
        for k in range(32):
            moneyness = mine[b + k] + other[b + k]
            held[b + k] = notional[b + k] * jax.nn.sigmoid(moneyness - strike[b + k]) * weight

    hand_out(idx, held, out, count)
    pltpu.make_async_copy(received, taken, sem).wait()


def value_and_hand_out(
    idx, mine, other, notional, strike, received, tiles, shards, count, weight
):
    scen = mine.shape[2]
    vmem = pl.BlockSpec(memory_space=pltpu.VMEM)
    hbm = pl.BlockSpec(memory_space=pl.ANY)
    return pl.pallas_call(
        functools.partial(value_and_hand_out_body, count=count, weight=weight),
        in_specs=[pl.BlockSpec(memory_space=pltpu.SMEM), vmem, vmem, vmem, vmem, hbm, hbm],
        out_specs=[vmem, vmem],
        out_shape=[
            jax.ShapeDtypeStruct((shards, count * SLICE, scen), jnp.bfloat16),
            jax.ShapeDtypeStruct(received.shape, jnp.bfloat16),
        ],
        scratch_shapes=[pltpu.VMEM(mine.shape, jnp.float32), pltpu.SemaphoreType.DMA],
        compiler_params=params(PASSING_LIMIT),
        name="value_and_hand_out",
    )(idx, mine, other, notional, strike, received, tiles)


def only_hand_out_body(idx, blocks, out, held, *, count):
    held[...] = blocks[...].astype(jnp.float32).reshape(held.shape)
    hand_out(idx, held, out, count)


def only_hand_out(idx, blocks, shards, count):
    scen = blocks.shape[2]
    vmem = pl.BlockSpec(memory_space=pltpu.VMEM)
    held = blocks.shape[0] * blocks.shape[1] // SLICE
    return pl.pallas_call(
        functools.partial(only_hand_out_body, count=count),
        in_specs=[pl.BlockSpec(memory_space=pltpu.SMEM), vmem],
        out_specs=vmem,
        out_shape=jax.ShapeDtypeStruct((shards, count * SLICE, scen), jnp.bfloat16),
        scratch_shapes=[pltpu.VMEM((held, SLICE, scen), jnp.float32)],
        compiler_params=params(),
        name="hand_out",
    )(idx, blocks)


def tile_grad_pair(grads, pair):
    rows = grads[:, 2 * SLICE * pair : 2 * SLICE * (pair + 1), :].astype(jnp.float32)
    width = rows.shape[0] * SLICE
    return [
        rows[:, u * SLICE : (u + 1) * SLICE, :].reshape(width, -1).astype(jnp.bfloat16)
        for u in range(2)
    ]


def first_backward_body(meta, grads, tiles, total):
    total[...] = jnp.zeros_like(total)
    for k in range(tiles.shape[0] // 2):
        for u, grad in enumerate(tile_grad_pair(grads, k)):
            product = jnp.dot(tiles[2 * k + u], grad, preferred_element_type=jnp.float32)
            total[meta[1 + 2 * k + u]] += product


def first_backward(meta, grads, tiles, blocks_dev):
    vmem = pl.BlockSpec(memory_space=pltpu.VMEM)
    return pl.pallas_call(
        first_backward_body,
        in_specs=[pl.BlockSpec(memory_space=pltpu.SMEM), vmem, vmem],
        out_specs=vmem,
        out_shape=jax.ShapeDtypeStruct(
            (blocks_dev, tiles.shape[1], grads.shape[2]), jnp.float32
        ),
        compiler_params=params(),
        name="first_backward",
    )(meta, grads, tiles)


def last_backward_body(meta, grads0, grads1, inputs, tiles, *rest, first):
    if first:
        earlier, _, sens, adjoint_out, *scratch, total, adjoint, adjoint_sem = rest
    else:
        sens, total, *scratch = rest
    grads, grads_sems, stage, out_sems, held, sems = scratch
    take = tile_copies(tiles, first, held, sems)

    pairs = stage.shape[0]

    def grads_copy(source, k):
        rows = slice(2 * SLICE * k, 2 * SLICE * (k + 1))
        return pltpu.make_async_copy(source.at[:, rows], grads.at[:, rows], grads_sems.at[k])

    @pl.when(meta[0] == 0)
    def _():
        for k in range(pairs):
            grads_copy(grads0, k).start()

    @pl.when(meta[0] == 1)
    def _():
        for k in range(pairs):
            grads_copy(grads1, k).start()

    for k in range(pairs):
        take(k).start()
    total[...] = earlier[...] if first else jnp.zeros_like(total)

    def put(k):
        return pltpu.make_async_copy(
            stage.at[k // 2, k % 2], sens.at[first + k], out_sems.at[k]
        )

    for k in range(pairs):
        take(k).wait()
        grads_copy(grads0, k).wait()
        for u, grad in enumerate(tile_grad_pair(grads, k)):
            col = meta[1 + first + 2 * k + u]
            total[col] += jnp.dot(held[2 * k + u], grad, preferred_element_type=jnp.float32)
            stage[k, u] = lax.dot_general(
                inputs[col], grad, (((1,), (1,)), ((), ())), preferred_element_type=jnp.float32
            ).astype(jnp.bfloat16)
            put(2 * k + u).start()

    if first:
        width = total.shape[1]
        for c in range(total.shape[0]):
            adjoint[:, c * width : (c + 1) * width] = total[c].T.astype(jnp.bfloat16)
        adjoint_copy = pltpu.make_async_copy(adjoint, adjoint_out, adjoint_sem)
        adjoint_copy.start()
        adjoint_copy.wait()
    for k in range(2 * pairs):
        put(k).wait()


def last_backward_calls(meta, grads, inputs, tiles):
    slots, width, _ = tiles.shape
    half = slots // 2
    blocks_dev, _, scen = inputs.shape
    smem = pl.BlockSpec(memory_space=pltpu.SMEM)
    vmem = pl.BlockSpec(memory_space=pltpu.VMEM)
    hbm = pl.BlockSpec(memory_space=pl.ANY)
    sens_shape = jax.ShapeDtypeStruct((slots, width, width), jnp.bfloat16)
    total_shape = jax.ShapeDtypeStruct(inputs.shape, jnp.float32)
    sems = pltpu.SemaphoreType.DMA((half // 2,))
    scratch = [
        pltpu.VMEM(grads[0][0].shape, jnp.bfloat16),
        sems,
        pltpu.VMEM((half // 2, 2, width, width), jnp.bfloat16),
        pltpu.SemaphoreType.DMA((half,)),
        *tile_scratch(half, width),
    ]
    adjoint_shape = (scen, blocks_dev * width)
    sens, total = pl.pallas_call(
        functools.partial(last_backward_body, first=0),
        in_specs=[smem, hbm, hbm, vmem, hbm],
        out_specs=[hbm, vmem],
        out_shape=[sens_shape, total_shape],
        scratch_shapes=scratch,
        compiler_params=params(STREAM_LIMIT),
        name="last_backward_low",
    )(meta, *grads[0], inputs, tiles)
    return pl.pallas_call(
        functools.partial(last_backward_body, first=half),
        in_specs=[smem, hbm, hbm, vmem, hbm, vmem, hbm],
        out_specs=[hbm, hbm],
        out_shape=[sens_shape, jax.ShapeDtypeStruct(adjoint_shape, jnp.bfloat16)],
        scratch_shapes=[
            *scratch,
            pltpu.VMEM(inputs.shape, jnp.float32),
            pltpu.VMEM(adjoint_shape, jnp.bfloat16),
            pltpu.SemaphoreType.DMA,
        ],
        input_output_aliases={6: 0},
        compiler_params=params(STREAM_LIMIT),
        name="last_backward_high",
    )(meta, *grads[1], inputs, tiles, total, sens)


def three_terms(values):
    terms = []
    for _ in range(3):
        term = lax.reduce_precision(values, 8, 7)
        terms.append(term)
        values = values - term
    return jnp.stack(terms)


def scales_to_send(notional, strike, shards, blocks_dev, scen):
    scales = jnp.stack([three_terms(notional), three_terms(strike)])
    scales = scales.reshape(6, blocks_dev, shards, SLICE).transpose(2, 0, 1, 3)
    scales = scales.reshape(shards, 1, 6 * blocks_dev * SLICE).astype(jnp.bfloat16)
    return jnp.pad(scales, ((0, 0), (0, SLICE - 1), (0, scen - scales.shape[2])))


def exchange(block):
    return lax.all_to_all(block, "blk", split_axis=0, concat_axis=0, tiled=True)


def on_device(normals, section_tile_list, tile_output_block, tile_col, notional, strike):
    shards = lax.axis_size("blk")
    core = lax.axis_index("phase")
    tiles = section_tile_list[0]
    slots, width, _ = tiles.shape
    half = slots // 2
    scen, local_width = normals.shape
    blocks_dev = local_width // width
    blocks = shards * blocks_dev
    cols = tile_col[0]
    weight = 1.0 / math.sqrt(scen)

    def of_core(zero, one):
        return jnp.where(core == 0, zero, one)

    def send(block, source):
        return lax.ppermute(block, "phase", [(source, 1 - source)])

    def swap(block):
        return lax.ppermute(block, "phase", [(0, 1), (1, 0)])

    my_places = jnp.concatenate([tile_output_block[0], cols])
    other_places = swap(my_places)
    places = [of_core(my_places, other_places), of_core(other_places, my_places)]
    split_rows = []
    for place in places:
        rows = place[: shards * slots].reshape(shards, slots)
        split_rows.append(of_core(rows[:, :half], rows[:, half:]).reshape(-1))
    my_number = core[None].astype(jnp.int32)
    split_meta = jnp.concatenate([my_number, of_core(places[1][-slots:-half], cols[half:])])
    meta = jnp.concatenate([my_number, cols])

    split = half // 4 + 1
    sent, low_tiles = first_products(tile_col, normals, tiles, half, half, range(split))
    kept, low_tiles = first_products(
        tile_col, normals, tiles, 0, half, range(split, half // 2), (low_tiles,)
    )
    arrived = exchange(of_core(kept, send(sent, 0)))
    scales = scales_to_send(notional, strike, shards, blocks_dev, scen)
    split_rows[0], scales, split_meta, meta = lax.optimization_barrier(
        (split_rows[0], scales, split_meta, meta)
    )
    part = add_up(split_rows[0], arrived, blocks)
    other_part, low_tiles = lax.optimization_barrier((swap(part), low_tiles))
    received = send(low_tiles, 1)
    shock_slices = (part + other_part).astype(jnp.bfloat16)

    shock_rows = shock_slices.reshape(shards, blocks_dev * SLICE, scen)
    arrived = exchange(jnp.concatenate([shock_rows, scales], axis=1))
    shocks = arrived[:, : blocks_dev * SLICE].reshape(shards, blocks_dev, SLICE, scen)
    shocks = shocks.transpose(1, 0, 2, 3).reshape(blocks_dev, width, scen)
    shocks_natural = shocks.transpose(2, 0, 1).reshape(scen, local_width)
    scales = arrived[:, blocks_dev * SLICE, : 6 * blocks_dev * SLICE].astype(jnp.float32)
    scales = scales.reshape(shards, 2, 3, blocks_dev, SLICE)
    scales = (scales[:, :, 0] + scales[:, :, 1]) + scales[:, :, 2]
    scales = scales.transpose(1, 0, 2, 3).reshape(2, blocks, SLICE, 1)

    arrived = exchange(split_products(split_meta, shocks_natural, received, tiles))
    split_rows[1], scales = lax.optimization_barrier((split_rows[1], scales))
    part = add_up(split_rows[1], arrived, blocks)
    outgoing, split_tiles = value_and_hand_out(
        split_rows[1],
        part,
        swap(part),
        scales[0],
        scales[1],
        received,
        tiles,
        shards,
        half,
        weight,
    )

    high1 = exchange(outgoing)
    part = first_backward(split_meta, high1, split_tiles, blocks_dev)
    shock_grad = (part + swap(part)).astype(jnp.bfloat16)
    low1 = send(high1, 0)

    shock_grad = shock_grad.reshape(blocks_dev, shards, SLICE, scen).transpose(1, 0, 2, 3)
    arrived = exchange(shock_grad.reshape(shards, blocks_dev * SLICE, scen))
    normals_held = normals.reshape(scen, blocks_dev, width).transpose(1, 2, 0)
    inputs = of_core(normals_held, shocks)
    low0 = exchange(only_hand_out(split_rows[0], arrived, shards, half))
    high0 = send(low0, 1)
    sens, adjoint = last_backward_calls(
        meta, ((low0, low1), (high0, high1)), inputs, tiles
    )
    return sens[None], adjoint[None]


def solution(mesh):
    return jax.shard_map(
        on_device,
        mesh=mesh,
        in_specs=(
            P(None, "blk"),
            P("phase", "blk", None, None),
            P("phase", None),
            P("phase", "blk"),
            P("blk"),
            P("blk"),
        ),
        out_specs=(P("phase", "blk", None, None), P("phase", None, "blk")),
        check_vma=False,
    )
```

```python
import functools
import math

import jax
import jax.numpy as jnp
from jax import lax
from jax.experimental import pallas as pl
from jax.experimental.pallas import tpu as pltpu
from jax.sharding import PartitionSpec as P

SLICE = 8
VMEM_LIMIT = 16 * 1024 * 1024
STREAM_LIMIT = 48 * 1024 * 1024
PASSING_LIMIT = 45 * 1024 * 1024


def params(limit=VMEM_LIMIT):
    return pltpu.CompilerParams(vmem_limit_bytes=limit)


def tile_copies(source, first, held, sems):
    def copy(k):
        return pltpu.make_async_copy(
            source.at[pl.ds(first + 2 * k, 2)], held.at[pl.ds(2 * k, 2)], sems.at[k]
        )

    return copy


def tile_scratch(count, width):
    return [pltpu.VMEM((count, width, width), jnp.bfloat16), pltpu.SemaphoreType.DMA((count // 2,))]


def product_pair(cols, at, x, tiles, out, pair):
    width = tiles.shape[1]
    parts = []
    for u in range(2):
        col = cols[at + 2 * pair + u]
        picked = x[:, pl.ds(pl.multiple_of(col * width, width), width)]
        product = jnp.dot(picked, tiles[2 * pair + u], preferred_element_type=jnp.float32)
        parts.append(product.T.reshape(width // SLICE, SLICE, x.shape[0]))
    both = jnp.concatenate(parts, axis=1).astype(jnp.bfloat16)
    out[:, 2 * SLICE * pair : 2 * SLICE * (pair + 1), :] = both


def put_rows(stage, out, sems, k):
    rows = slice(2 * SLICE * k, 2 * SLICE * (k + 1))
    return pltpu.make_async_copy(stage.at[:, rows], out.at[:, rows], sems.at[k])


def first_products_body(cols_in, x_in, tiles, *rest, first, moved):
    out, low, cols, x, small_sems, held, sems, low_sems = rest[-8:]
    pairs = held.shape[0] // 2
    core = lax.axis_index("phase")

    @pl.when(core == 0)
    def _():
        copy = tile_copies(tiles, first, held, sems)
        cols_copy = pltpu.make_async_copy(cols_in, cols, small_sems.at[0])
        x_copy = pltpu.make_async_copy(x_in, x, small_sems.at[1])
        cols_copy.start()
        x_copy.start()
        for k in range(pairs):
            copy(k).start()
        cols_copy.wait()
        x_copy.wait()
        for k in range(pairs):
            copy(k).wait()
            product_pair(cols.at[0], first, x, held, out, k)

    @pl.when(core == 1)
    def _():
        copy = tile_copies(tiles, 0, held, sems)

        def put(k):
            return pltpu.make_async_copy(
                held.at[pl.ds(2 * k, 2)], low.at[pl.ds(2 * k, 2)], low_sems.at[k]
            )

        for k in moved:
            copy(k).start()
        for k in moved:
            copy(k).wait()
            put(k).start()
        for k in moved:
            put(k).wait()


def first_products(cols, x, tiles, first, count, moved, low=()):
    width = tiles.shape[1]
    scen = x.shape[0]
    vmem = pl.BlockSpec(memory_space=pltpu.VMEM)
    hbm = pl.BlockSpec(memory_space=pl.ANY)
    return pl.pallas_call(
        functools.partial(first_products_body, first=first, moved=moved),
        in_specs=[hbm] * (3 + len(low)),
        out_specs=[vmem, hbm],
        out_shape=[
            jax.ShapeDtypeStruct((width // SLICE, count * SLICE, scen), jnp.bfloat16),
            jax.ShapeDtypeStruct((count, width, width), jnp.bfloat16),
        ],
        scratch_shapes=[
            pltpu.SMEM(cols.shape, jnp.int32),
            pltpu.VMEM(x.shape, jnp.bfloat16),
            pltpu.SemaphoreType.DMA((2,)),
        ]
        + tile_scratch(count, width)
        + [pltpu.SemaphoreType.DMA((count // 2,))],
        input_output_aliases={3: 1} if low else {},
        compiler_params=params(STREAM_LIMIT),
        name="first_products",
    )(cols, x, tiles, *low)


def start_split_tiles(core, received, tiles, held, sems):
    count = held.shape[0]

    @pl.when(core == 0)
    def _():
        for k in range(count // 2):
            tile_copies(received, 0, held, sems)(k).start()

    @pl.when(core == 1)
    def _():
        for k in range(count // 2):
            tile_copies(tiles, count, held, sems)(k).start()

    return tile_copies(received, 0, held, sems)


def split_products_body(meta, x, received, tiles, out, held, sems, stage, out_sems):
    pairs = held.shape[0] // 2
    copy = start_split_tiles(meta[0], received, tiles, held, sems)

    for k in range(pairs):
        copy(k).wait()
        product_pair(meta, 1, x, held, stage, k)
        put_rows(stage, out, out_sems, k).start()
    for k in range(pairs):
        put_rows(stage, out, out_sems, k).wait()


def split_products(meta, x, received, tiles):
    count, width = received.shape[0], received.shape[1]
    out_shape = (width // SLICE, count * SLICE, x.shape[0])
    vmem = pl.BlockSpec(memory_space=pltpu.VMEM)
    hbm = pl.BlockSpec(memory_space=pl.ANY)
    return pl.pallas_call(
        split_products_body,
        in_specs=[pl.BlockSpec(memory_space=pltpu.SMEM), vmem, hbm, hbm],
        out_specs=hbm,
        out_shape=jax.ShapeDtypeStruct(out_shape, jnp.bfloat16),
        scratch_shapes=tile_scratch(count, width)
        + [pltpu.VMEM(out_shape, jnp.bfloat16), pltpu.SemaphoreType.DMA((count // 2,))],
        compiler_params=params(STREAM_LIMIT),
        name="split_products",
    )(meta, x, received, tiles)


def add_up_body(idx, data, out, second, *, count):
    out[...] = jnp.zeros_like(out)
    second[...] = jnp.zeros_like(second)

    @pl.loop(0, data.shape[0], step=2)
    def _(i):
        for holder, total in ((i, out), (i + 1, second)):
            values = data[holder].astype(jnp.float32)
            places = [idx[holder * count + t] for t in range(count)]
            sums = [
                total[places[t]] + values[t * SLICE : (t + 1) * SLICE] for t in range(count)
            ]
            for t in range(count):
                total[places[t]] = sums[t]

    out[...] += second[...]


def add_up(idx, data, blocks):
    count = data.shape[1] // SLICE
    return pl.pallas_call(
        functools.partial(add_up_body, count=count),
        in_specs=[pl.BlockSpec(memory_space=pltpu.SMEM), pl.BlockSpec(memory_space=pltpu.VMEM)],
        out_specs=pl.BlockSpec(memory_space=pltpu.VMEM),
        out_shape=jax.ShapeDtypeStruct((blocks, SLICE, data.shape[2]), jnp.float32),
        scratch_shapes=[pltpu.VMEM((blocks, SLICE, data.shape[2]), jnp.float32)],
        compiler_params=params(),
        name="add_up",
    )(idx, data)


def hand_out(idx, held, out, count):
    @pl.loop(0, out.shape[0], step=4)
    def _(i):
        for holder in (i, i + 1, i + 2, i + 3):
            for t in range(0, count, 2):
                pair = [held[idx[holder * count + t]], held[idx[holder * count + t + 1]]]
                rows = jnp.concatenate(pair, axis=0).astype(jnp.bfloat16)
                out[holder, t * SLICE : (t + 2) * SLICE, :] = rows


def value_and_hand_out_body(
    idx, mine, other, notional, strike, received, tiles, out, taken, held, sem, *, count, weight
):
    core = lax.axis_index("phase")
    half = taken.shape[0]

    @pl.when(core == 0)
    def _():
        pltpu.make_async_copy(received, taken, sem).start()

    @pl.when(core == 1)
    def _():
        pltpu.make_async_copy(tiles.at[pl.ds(half, half)], taken, sem).start()

    @pl.loop(0, held.shape[0], step=32)
    def _(b):
        for k in range(32):
            moneyness = mine[b + k] + other[b + k]
            held[b + k] = notional[b + k] * jax.nn.sigmoid(moneyness - strike[b + k]) * weight

    hand_out(idx, held, out, count)
    pltpu.make_async_copy(received, taken, sem).wait()


def value_and_hand_out(
    idx, mine, other, notional, strike, received, tiles, shards, count, weight
):
    scen = mine.shape[2]
    vmem = pl.BlockSpec(memory_space=pltpu.VMEM)
    hbm = pl.BlockSpec(memory_space=pl.ANY)
    return pl.pallas_call(
        functools.partial(value_and_hand_out_body, count=count, weight=weight),
        in_specs=[pl.BlockSpec(memory_space=pltpu.SMEM), vmem, vmem, vmem, vmem, hbm, hbm],
        out_specs=[vmem, vmem],
        out_shape=[
            jax.ShapeDtypeStruct((shards, count * SLICE, scen), jnp.bfloat16),
            jax.ShapeDtypeStruct(received.shape, jnp.bfloat16),
        ],
        scratch_shapes=[pltpu.VMEM(mine.shape, jnp.float32), pltpu.SemaphoreType.DMA],
        compiler_params=params(PASSING_LIMIT),
        name="value_and_hand_out",
    )(idx, mine, other, notional, strike, received, tiles)


def only_hand_out_body(idx, blocks, out, held, *, count):
    held[...] = blocks[...].astype(jnp.float32).reshape(held.shape)
    hand_out(idx, held, out, count)


def only_hand_out(idx, blocks, shards, count):
    scen = blocks.shape[2]
    vmem = pl.BlockSpec(memory_space=pltpu.VMEM)
    held = blocks.shape[0] * blocks.shape[1] // SLICE
    return pl.pallas_call(
        functools.partial(only_hand_out_body, count=count),
        in_specs=[pl.BlockSpec(memory_space=pltpu.SMEM), vmem],
        out_specs=vmem,
        out_shape=jax.ShapeDtypeStruct((shards, count * SLICE, scen), jnp.bfloat16),
        scratch_shapes=[pltpu.VMEM((held, SLICE, scen), jnp.float32)],
        compiler_params=params(),
        name="hand_out",
    )(idx, blocks)


def tile_grad_pair(grads, pair):
    rows = grads[:, 2 * SLICE * pair : 2 * SLICE * (pair + 1), :].astype(jnp.float32)
    width = rows.shape[0] * SLICE
    return [
        rows[:, u * SLICE : (u + 1) * SLICE, :].reshape(width, -1).astype(jnp.bfloat16)
        for u in range(2)
    ]


def first_backward_body(meta, grads, tiles, total):
    total[...] = jnp.zeros_like(total)
    for k in range(tiles.shape[0] // 2):
        for u, grad in enumerate(tile_grad_pair(grads, k)):
            product = jnp.dot(tiles[2 * k + u], grad, preferred_element_type=jnp.float32)
            total[meta[1 + 2 * k + u]] += product


def first_backward(meta, grads, tiles, blocks_dev):
    vmem = pl.BlockSpec(memory_space=pltpu.VMEM)
    return pl.pallas_call(
        first_backward_body,
        in_specs=[pl.BlockSpec(memory_space=pltpu.SMEM), vmem, vmem],
        out_specs=vmem,
        out_shape=jax.ShapeDtypeStruct(
            (blocks_dev, tiles.shape[1], grads.shape[2]), jnp.float32
        ),
        compiler_params=params(),
        name="first_backward",
    )(meta, grads, tiles)


def last_backward_body(
    meta, low0, low1, high0, high1, inputs, tiles, sens, adjoint_out, *scratch
):
    grads, grads_sems, stage, out_sems, held, sems, total, adjoint, adjoint_sem = scratch
    pairs = stage.shape[0]
    half = pairs // 2
    take = tile_copies(tiles, 0, held, sems)

    def grads_copy(source, k):
        rows = slice(2 * SLICE * (k % half), 2 * SLICE * (k % half + 1))
        return pltpu.make_async_copy(
            source.at[:, rows], grads.at[k // half, :, rows], grads_sems.at[k]
        )

    def put(k):
        return pltpu.make_async_copy(stage.at[k // 2, k % 2], sens.at[k], out_sems.at[k])

    for section, halves in ((0, (low0, high0)), (1, (low1, high1))):

        @pl.when(meta[0] == section)
        def _(halves=halves):
            for k in range(pairs):
                grads_copy(halves[k // half], k).start()
                take(k).start()

    total[...] = jnp.zeros_like(total)
    for k in range(pairs):
        take(k).wait()
        grads_copy(low0, k).wait()
        for u, grad in enumerate(tile_grad_pair(grads.at[k // half], k % half)):
            col = meta[1 + 2 * k + u]
            total[col] += jnp.dot(held[2 * k + u], grad, preferred_element_type=jnp.float32)
            stage[k, u] = lax.dot_general(
                inputs[col], grad, (((1,), (1,)), ((), ())), preferred_element_type=jnp.float32
            ).astype(jnp.bfloat16)
            put(2 * k + u).start()

    width = total.shape[1]
    for c in range(total.shape[0]):
        adjoint[:, c * width : (c + 1) * width] = total[c].T.astype(jnp.bfloat16)
    adjoint_copy = pltpu.make_async_copy(adjoint, adjoint_out, adjoint_sem)
    adjoint_copy.start()
    adjoint_copy.wait()
    for k in range(2 * pairs):
        put(k).wait()


def last_backward(meta, low0, low1, high0, high1, inputs, tiles):
    slots, width, _ = tiles.shape
    blocks_dev, _, scen = inputs.shape
    hbm = pl.BlockSpec(memory_space=pl.ANY)
    adjoint_shape = (scen, blocks_dev * width)
    return pl.pallas_call(
        last_backward_body,
        in_specs=[pl.BlockSpec(memory_space=pltpu.SMEM)]
        + [hbm] * 4
        + [pl.BlockSpec(memory_space=pltpu.VMEM), hbm],
        out_specs=[hbm, hbm],
        out_shape=[
            jax.ShapeDtypeStruct(tiles.shape, jnp.bfloat16),
            jax.ShapeDtypeStruct(adjoint_shape, jnp.bfloat16),
        ],
        scratch_shapes=[
            pltpu.VMEM((2, *low0.shape), jnp.bfloat16),
            pltpu.SemaphoreType.DMA((slots // 2,)),
            pltpu.VMEM((slots // 2, 2, width, width), jnp.bfloat16),
            pltpu.SemaphoreType.DMA((slots,)),
            *tile_scratch(slots, width),
            pltpu.VMEM(inputs.shape, jnp.float32),
            pltpu.VMEM(adjoint_shape, jnp.bfloat16),
            pltpu.SemaphoreType.DMA,
        ],
        compiler_params=params(STREAM_LIMIT),
        name="last_backward",
    )(meta, low0, low1, high0, high1, inputs, tiles)


def three_terms(values):
    terms = []
    for _ in range(3):
        term = lax.reduce_precision(values, 8, 7)
        terms.append(term)
        values = values - term
    return jnp.stack(terms)


def scales_to_send(notional, strike, shards, blocks_dev, scen):
    scales = jnp.stack([three_terms(notional), three_terms(strike)])
    scales = scales.reshape(6, blocks_dev, shards, SLICE).transpose(2, 0, 1, 3)
    scales = scales.reshape(shards, 1, 6 * blocks_dev * SLICE).astype(jnp.bfloat16)
    return jnp.pad(scales, ((0, 0), (0, SLICE - 1), (0, scen - scales.shape[2])))


def exchange(block):
    return lax.all_to_all(block, "blk", split_axis=0, concat_axis=0, tiled=True)


def on_device(normals, section_tile_list, tile_output_block, tile_col, notional, strike):
    shards = lax.axis_size("blk")
    core = lax.axis_index("phase")
    tiles = section_tile_list[0]
    slots, width, _ = tiles.shape
    half = slots // 2
    scen, local_width = normals.shape
    blocks_dev = local_width // width
    blocks = shards * blocks_dev
    cols = tile_col[0]
    weight = 1.0 / math.sqrt(scen)

    def of_core(zero, one):
        return jnp.where(core == 0, zero, one)

    def send(block, source):
        return lax.ppermute(block, "phase", [(source, 1 - source)])

    def swap(block):
        return lax.ppermute(block, "phase", [(0, 1), (1, 0)])

    my_places = jnp.concatenate([tile_output_block[0], cols])
    other_places = swap(my_places)
    places = [of_core(my_places, other_places), of_core(other_places, my_places)]
    split_rows = []
    for place in places:
        rows = place[: shards * slots].reshape(shards, slots)
        split_rows.append(of_core(rows[:, :half], rows[:, half:]).reshape(-1))
    my_number = core[None].astype(jnp.int32)
    split_meta = jnp.concatenate([my_number, of_core(places[1][-slots:-half], cols[half:])])
    meta = jnp.concatenate([my_number, cols])

    split = half // 4 + 1
    sent, low_tiles = first_products(tile_col, normals, tiles, half, half, range(split))
    kept, low_tiles = first_products(
        tile_col, normals, tiles, 0, half, range(split, half // 2), (low_tiles,)
    )
    arrived = exchange(of_core(kept, send(sent, 0)))
    scales = scales_to_send(notional, strike, shards, blocks_dev, scen)
    split_rows[0], scales, split_meta, meta = lax.optimization_barrier(
        (split_rows[0], scales, split_meta, meta)
    )
    part = add_up(split_rows[0], arrived, blocks)
    other_part, low_tiles = lax.optimization_barrier((swap(part), low_tiles))
    received = send(low_tiles, 1)
    shock_slices = (part + other_part).astype(jnp.bfloat16)

    shock_rows = shock_slices.reshape(shards, blocks_dev * SLICE, scen)
    arrived = exchange(jnp.concatenate([shock_rows, scales], axis=1))
    shocks = arrived[:, : blocks_dev * SLICE].reshape(shards, blocks_dev, SLICE, scen)
    shocks = shocks.transpose(1, 0, 2, 3).reshape(blocks_dev, width, scen)
    shocks_natural = shocks.transpose(2, 0, 1).reshape(scen, local_width)
    scales = arrived[:, blocks_dev * SLICE, : 6 * blocks_dev * SLICE].astype(jnp.float32)
    scales = scales.reshape(shards, 2, 3, blocks_dev, SLICE)
    scales = (scales[:, :, 0] + scales[:, :, 1]) + scales[:, :, 2]
    scales = scales.transpose(1, 0, 2, 3).reshape(2, blocks, SLICE, 1)

    arrived = exchange(split_products(split_meta, shocks_natural, received, tiles))
    split_rows[1], scales = lax.optimization_barrier((split_rows[1], scales))
    part = add_up(split_rows[1], arrived, blocks)
    outgoing, split_tiles = value_and_hand_out(
        split_rows[1],
        part,
        swap(part),
        scales[0],
        scales[1],
        received,
        tiles,
        shards,
        half,
        weight,
    )

    high1 = exchange(outgoing)
    part = first_backward(split_meta, high1, split_tiles, blocks_dev)
    shock_grad = (part + swap(part)).astype(jnp.bfloat16)
    low1 = send(high1, 0)

    shock_grad = shock_grad.reshape(blocks_dev, shards, SLICE, scen).transpose(1, 0, 2, 3)
    arrived = exchange(shock_grad.reshape(shards, blocks_dev * SLICE, scen))
    normals_held = normals.reshape(scen, blocks_dev, width).transpose(1, 2, 0)
    inputs = of_core(normals_held, shocks)
    low0 = exchange(only_hand_out(split_rows[0], arrived, shards, half))
    high0 = send(low0, 1)
    sens, adjoint = last_backward(meta, low0, low1, high0, high1, inputs, tiles)
    return sens[None], adjoint[None]


def solution(mesh):
    return jax.shard_map(
        on_device,
        mesh=mesh,
        in_specs=(
            P(None, "blk"),
            P("phase", "blk", None, None),
            P("phase", None),
            P("phase", "blk"),
            P("blk"),
            P("blk"),
        ),
        out_specs=(P("phase", "blk", None, None), P("phase", None, "blk")),
        check_vma=False,
    )
```
